256 devices in a mesh: dp: 8 (over y, core), mp: 32 (over x, z).
Axes of the slice: x: 4, y: 4, z: 8, core: 2. Of those that a mesh axis runs over, the one named last changes fastest.
Arguments:
- tokens: bfloat16 [1024, 8192], P('dp', 'mp'), may hold values from -6 to 6
- cotangent: bfloat16 [1024, 28672], P('dp', 'mp'), may hold values from -2 to 2
- tiles: bfloat16 [2, 1344, 128, 128], P(None, 'mp'), may hold values from -0.1875 to 0.1875
- tile_rows: int32 [2, 1344], replicated, may hold values from 0 to 63, as said below
- tile_cols: int32 [2, 1344], replicated, may hold values from 0 to 223, as said below
Outputs:
- hidden: bfloat16 [1024, 28672], P('dp', 'mp')
- input_grad: bfloat16 [1024, 8192], P('dp', 'mp')
- tile_grads: float32 [2, 1344, 128, 128], P(None, 'mp')
The draws below stay inside these ranges and needn't reach their ends.
Inputs may be any that keep to these rules, and one draw needn't show every extreme that they name: `tile_rows`: row m lists the tiles of matrix m; device k // 42 of mp owns tile k. Within one column panel of one matrix the row blocks are distinct. `tile_cols`: A column panel holds 12 or 4 tiles, the same count for all 7 panels of one holder (panels c with equal c // 7), 12 for a quarter of the holders. An owner's tiles are listed in the order of their panels. At most 3 of one owner's tiles of a matrix lie in one holder's panels, and this bound is reached in every matrix.
All inputs are finite; a program needn't handle non-finite values.
Results may differ from the reference program's by a relative error of at most 0.02.
Values may be sent and summed in bfloat16 or wider, within the bound.
No kernel may reach another device: no remote copies, remote signals or barrier semaphores. Data moves between devices by JAX's collectives and lax.ppermute only.
A program may use at most 128 MiB of HBM per device.

```python
import jax
import jax.numpy as jnp
from jax import lax

D = 8192
FF = 28672
BLOCK = 128
KHEAVY = 12
KLIGHT = 4
GTOK = 128
RB = 64
CB = 224
NT = 1344
TOKENS = 1024
N_DP = 8
N_MP = 32


def mask_layout(key, matrix):
    key = jax.random.fold_in(key, 100 + matrix)
    holder_key, order_key, owner_key = jax.random.split(key, 3)
    panel_count = FF // BLOCK
    per_holder = panel_count // N_MP
    owned_count = per_holder * (KHEAVY + 3 * KLIGHT) // 4
    listed = owned_count * N_MP
    holder_rank = jax.random.permutation(holder_key, N_MP)
    heavy = holder_rank < N_MP // 4
    counts = jnp.where(heavy[jnp.arange(panel_count) // per_holder], KHEAVY, KLIGHT).astype(jnp.int32)
    ends = jnp.cumsum(counts)
    position = jnp.arange(listed, dtype=jnp.int32)
    column = jnp.sum((ends[None, :] <= position[:, None]).astype(jnp.int32), axis=1)
    within = position - (ends[column] - counts[column])
    orders = jax.vmap(lambda sub_key: jax.random.permutation(sub_key, D // BLOCK))(jax.random.split(order_key, panel_count))
    row = orders[column, within].astype(jnp.int32)
    owner_perm = jax.random.permutation(owner_key, N_MP)
    residue = jnp.argsort(owner_perm).astype(jnp.int32)
    layout = (residue[:, None] + N_MP * jnp.arange(owned_count, dtype=jnp.int32)[None, :]).reshape(-1)
    return (row[layout], column[layout])


def draw_tile_rows(key, part):
    shared = [mask_layout(key, matrix) for matrix in range(2)]
    return jnp.stack([shared[0][0], shared[1][0]]).astype(jnp.int32)


def draw_tile_cols(key, part):
    shared = [mask_layout(key, matrix) for matrix in range(2)]
    return jnp.stack([shared[0][1], shared[1][1]]).astype(jnp.int32)


def level_of(own_key, extent, cuts, least, top_value):
    level = 1.0
    for dim, parts in cuts:
        steps = jax.random.uniform(jax.random.fold_in(jax.random.fold_in(own_key, 6), dim), (parts,), jnp.float32, least / len(cuts), top_value / len(cuts))
        level = level * jnp.repeat(jnp.exp(steps), extent[dim] // parts).reshape((-1,) + (1,) * (len(extent) - 1 - dim))
    return level


def gaussian(own_key, extent, scale, most, cuts=(), held_as=jnp.bfloat16):
    level = level_of(own_key, extent, cuts, -0.22, 0.18) if cuts else 1.0
    values = jax.random.normal(own_key, extent, jnp.float32) * scale * level
    return jnp.minimum(jnp.maximum(values, -most), most).astype(held_as)


def setup_inputs(seed: int = 0) -> dict:
    key_list = jax.random.split(jax.random.key(seed), 6)
    tokens = gaussian(key_list[0], (TOKENS, D), 1.0, 6.0, ((0, 8), (1, 32)))
    cotangent = gaussian(key_list[1], (TOKENS, FF), 0.25, 2.0, ((0, 8), (1, 32)))
    tiles = gaussian(key_list[2], (2, NT, BLOCK, BLOCK), (8 * BLOCK) ** -0.5, 0.1875, ((1, 32),))
    tile_rows = draw_tile_rows(jax.random.fold_in(key_list[5], 71), 0)
    tile_cols = draw_tile_cols(jax.random.fold_in(key_list[5], 71), 0)
    return dict(tokens=tokens, cotangent=cotangent, tiles=tiles, tile_rows=tile_rows, tile_cols=tile_cols)


def reference(tokens, cotangent, tiles, tile_rows, tile_cols):
    weights = tiles.astype(jnp.float32)
    grad_total = jnp.zeros((2, NT, BLOCK, BLOCK), jnp.float32)
    hidden_parts = []
    input_parts = []
    for group_index in range(N_DP):
        low = group_index * GTOK
        group_tokens = tokens[low:low + GTOK].astype(jnp.float32).reshape(GTOK, RB, BLOCK)
        upstream = cotangent[low:low + GTOK].astype(jnp.float32)
        projected = []
        picked = []
        for matrix in range(2):
            chosen = group_tokens[:, tile_rows[matrix]]
            partial_value = jnp.einsum("nti,tij->ntj", chosen, weights[matrix], precision=lax.Precision.HIGHEST)
            summed = jnp.zeros((GTOK, CB, BLOCK), jnp.float32).at[:, tile_cols[matrix]].add(partial_value)
            projected.append(summed.reshape(GTOK, FF))
            picked.append(chosen)
        gate_pre, up_pre = projected
        sigmoid_gate = jax.nn.sigmoid(gate_pre)
        hidden_parts.append((gate_pre * sigmoid_gate * up_pre).astype(jnp.bfloat16))
        gate_grad = (upstream * up_pre * sigmoid_gate * (1.0 + gate_pre * (1.0 - sigmoid_gate))).astype(jnp.bfloat16)
        up_grad = (upstream * gate_pre * sigmoid_gate).astype(jnp.bfloat16)
        input_terms = jnp.zeros((GTOK, RB, BLOCK), jnp.float32)
        for matrix, grad_panel in enumerate((gate_grad, up_grad)):
            panel_cols = grad_panel.astype(jnp.float32).reshape(GTOK, CB, BLOCK)[:, tile_cols[matrix]]
            group_grad = jnp.einsum("nti,ntj->tij", picked[matrix], panel_cols, precision=lax.Precision.HIGHEST)
            rounded = lax.optimization_barrier(group_grad.astype(jnp.bfloat16))
            grad_total = grad_total.at[matrix].add(rounded.astype(jnp.float32))
            back_terms = jnp.einsum("ntj,tij->nti", panel_cols, weights[matrix], precision=lax.Precision.HIGHEST)
            input_terms = input_terms.at[:, tile_rows[matrix]].add(back_terms)
        input_parts.append(input_terms.reshape(GTOK, D).astype(jnp.bfloat16))
    return jnp.concatenate(hidden_parts, axis=0), jnp.concatenate(input_parts, axis=0), grad_total
```

```python
import jax
import jax.numpy as jnp
from jax import lax
from jax.experimental import pallas as pl
from jax.experimental.pallas import tpu as pltpu
from jax.sharding import PartitionSpec as P

BLOCK = 128
MOST = 12
PAIR = 3
GROUP = 4
F32 = jnp.float32
BF16 = jnp.bfloat16


def nt(a, b):
    return lax.dot_general(a, b, (((1,), (1,)), ((), ())), preferred_element_type=F32)


def nn(a, b):
    return lax.dot_general(a, b, (((1,), (0,)), ((), ())), preferred_element_type=F32)


def slot_table(tile_rows, tile_cols, me, members, panels):
    owned = tile_cols.shape[1] // members
    cols = tile_cols.reshape(2, members, owned)
    rows = tile_rows.reshape(2, members, owned)
    local = cols - me * panels
    holder = cols // panels
    pad = jnp.full((2, members, 2), -1, jnp.int32)

    def run(values):
        one = jnp.concatenate([pad[:, :, :1], values[:, :, :-1]], axis=2)
        two = jnp.concatenate([pad, values[:, :, :-2]], axis=2)
        return (values == one).astype(jnp.int32) + (values == two).astype(jnp.int32)

    rank = run(holder)
    within = run(cols)
    place = (
        jnp.arange(members)[None, :, None] * (2 * PAIR)
        + jnp.arange(2)[:, None, None] * PAIR
        + rank
    )
    value = place * 64 + rows
    mine = local[None] == jnp.arange(panels)[:, None, None, None]
    count = jnp.sum(mine.astype(jnp.int32), axis=3)
    before = jnp.arange(members)[:, None] > jnp.arange(members)[None, :]
    earlier = jnp.sum(jnp.where(before, count[:, :, None, :], 0), axis=3)
    place_in_panel = jnp.where(mine, earlier[..., None] + within[None], -1)
    hit = place_in_panel[:, :, None] == jnp.arange(MOST)[:, None, None]
    table = jnp.sum(jnp.where(hit, value[None, :, None], 0), axis=(3, 4))
    return table.reshape(-1), jnp.sum(count, axis=2).reshape(-1)


def slot_of(cols_ref, me, owned, panels, visit):
    for m in range(2):

        def step(k, carry):
            last, rank = carry
            holder = cols_ref[m, me * owned + k] // panels
            rank = jnp.where(holder == last, rank + 1, 0)
            visit(m, k, holder * (2 * PAIR) + m * PAIR + rank)
            return holder, rank

        lax.fori_loop(0, owned, step, (jnp.int32(-1), jnp.int32(0)), unroll=6)


def send_kernel(panels, place_ref, cols_ref, tiles_ref, tokens_ref, out_ref, blocks_ref):
    owned = tiles_ref.shape[1]

    def visit(m, k, slot):
        out_ref[slot] = tiles_ref[m, k]

    slot_of(cols_ref, place_ref[0], owned, panels, visit)
    for b in range(blocks_ref.shape[0]):
        blocks_ref[b] = tokens_ref[:, b * BLOCK : (b + 1) * BLOCK]


def own_kernel(panels, place_ref, cols_ref, back_ref, out_ref):
    owned = out_ref.shape[1]

    def visit(m, k, slot):
        out_ref[m, k] = back_ref[slot]

    slot_of(cols_ref, place_ref[0], owned, panels, visit)


def sort_kernel(table_ref, in_ref, out_ref):
    def step(s, carry):
        out_ref[s] = in_ref[table_ref[s] >> 6]
        return carry

    lax.fori_loop(0, out_ref.shape[0], step, 0, unroll=8)


def unsort_kernel(table_ref, count_ref, in_ref, out_ref):
    for q in range(in_ref.shape[0] // MOST):

        def step(t, carry):
            s = q * MOST + t
            out_ref[table_ref[s] >> 6] = in_ref[s]
            return carry

        lax.fori_loop(0, count_ref[q], step, 0)


def main_kernel(
    sides,
    table_ref,
    count_ref,
    where_ref,
    *refs,
):
    pieces, (tile_ref, cot_ref, hidden_ref, grad_ref) = refs[:sides], refs[sides : sides + 4]
    terms = refs[sides + 4 : 2 * sides + 4]
    tok_ref, tok_t, total, sems = refs[2 * sides + 4 :]
    p = pl.program_id(0)
    blocks = tok_ref.shape[0]
    each = blocks // sides
    side = where_ref[2]

    @pl.when(p == 0)
    def _():
        ring = pieces[0].shape[0]
        copies = [
            pltpu.make_async_copy(
                piece.at[j],
                tok_ref.at[
                    pl.ds(
                        lax.rem(side + sides - s, sides) * each
                        + lax.rem(where_ref[3] + ring - j, ring) * (each // ring),
                        each // ring,
                    )
                ],
                sems.at[s, j],
            )
            for s, piece in enumerate(pieces)
            for j in range(ring)
        ]
        for copy in copies:
            copy.start()
        for copy in copies:
            copy.wait()

        def step(b, carry):
            tok_t[b] = tok_ref[b].T
            total[b] = jnp.zeros_like(total[b])
            return carry

        lax.fori_loop(0, blocks, step, 0)

    def work(counts):
        at = [
            [table_ref[(p * 2 + m) * MOST + t] & 63 for t in range(counts[m])] for m in range(2)
        ]

        def weights(m, first):
            return tile_ref[:, m * MOST + first : m * MOST + first + GROUP]

        def stacked(m, first):
            w = weights(m, first)
            return jnp.concatenate([w[:, i].reshape(BLOCK, BLOCK) for i in range(GROUP)], axis=0)

        pre = []
        for m in range(2):
            acc = None
            for first in range(0, counts[m], GROUP):
                lhs = jnp.concatenate([tok_ref[at[m][first + i]] for i in range(GROUP)], axis=1)
                term = nn(lhs, stacked(m, first))
                acc = term if acc is None else acc + term
            pre.append(acc)
        gate, up = pre
        sig = 1.0 / (1.0 + jnp.exp(-gate))
        hidden_ref[...] = (gate * sig * up).astype(BF16)
        cot = cot_ref[...].astype(F32)
        grads = (
            (cot * up * sig * (1.0 + gate * (1.0 - sig))).astype(BF16),
            (cot * gate * sig).astype(BF16),
        )
        for m in range(2):
            for first in range(0, counts[m], GROUP):
                lhs = jnp.concatenate([tok_t[at[m][first + i]] for i in range(GROUP)], axis=0)
                out = nn(lhs, grads[m]).astype(BF16)
                back = nt(grads[m], stacked(m, first))
                for i in range(GROUP):
                    part = out[i * BLOCK : (i + 1) * BLOCK]
                    grad_ref[:, m * MOST + first + i] = part.reshape(8, BLOCK // 8, BLOCK)
                    total[at[m][first + i]] += back[:, i * BLOCK : (i + 1) * BLOCK]

    many = [count_ref[p * 2 + m] > GROUP for m in range(2)]
    for most in range(4):
        picked = [bool(most & 1), bool(most & 2)]
        same = [many[m] if picked[m] else jnp.logical_not(many[m]) for m in range(2)]

        @pl.when(jnp.logical_and(same[0], same[1]))
        def _():
            work([MOST if picked[m] else GROUP for m in range(2)])

    @pl.when(p == pl.num_programs(0) - 1)
    def _():
        for s in range(sides):
            base = lax.rem(side + s, sides) * each

            def step(b, carry):
                terms[s][b] = total[base + b].astype(BF16)
                return carry

            lax.fori_loop(0, each, step, 0)


def sum_kernel(in_ref, out_ref):
    def step(k, acc):
        return tuple(a + in_ref[k, i].astype(F32) for i, a in enumerate(acc))

    count = in_ref.shape[1]
    acc = lax.fori_loop(
        0, in_ref.shape[0], step, tuple(jnp.zeros(in_ref.shape[2:], F32) for _ in range(count))
    )
    for i in range(count):
        out_ref[:, i * BLOCK : (i + 1) * BLOCK] = acc[i].astype(BF16)


def add_kernel(*refs):
    out_ref = refs[-1]

    def step(b, carry):
        out_ref[b] = sum(r[b].astype(F32) for r in refs[:-1]).astype(BF16)
        return carry

    lax.fori_loop(0, out_ref.shape[0], step, 0)


def widen_kernel(in_ref, out_ref):
    parts, count, part, _ = in_ref.shape

    def step(i, carry):
        out_ref[i] = in_ref[:, i].reshape(parts * part, BLOCK).astype(F32)
        return carry

    lax.fori_loop(0, count, step, 0, unroll=2)


def whole(shape):
    return pl.BlockSpec(shape, lambda *_: (0,) * len(shape))


def per_device(tokens, cotangent, tiles, tile_rows, tile_cols):
    groups = lax.axis_size("dp")
    members = lax.axis_size("mp")
    me = lax.axis_index("mp")
    mygroup = lax.axis_index("dp")
    owned = tiles.shape[1]
    tok_rows, my_features = tokens.shape
    my_blocks = my_features // BLOCK
    row_blocks = my_blocks * members
    panels = cotangent.shape[1] // BLOCK
    part = BLOCK // groups
    slots = members * 2 * PAIR
    used = panels * 2 * MOST
    params = pltpu.CompilerParams(vmem_limit_bytes=48 * 1024 * 1024)
    sides = 4
    ring = members // sides
    each = row_blocks // sides
    where = jnp.stack([me, mygroup, me // ring, me % ring]).astype(jnp.int32)

    outgoing, my_tok = pl.pallas_call(
        lambda *refs: send_kernel(panels, *refs),
        out_shape=(
            jax.ShapeDtypeStruct((slots, part, BLOCK), BF16),
            jax.ShapeDtypeStruct((my_blocks, tok_rows, BLOCK), BF16),
        ),
        grid_spec=pltpu.PrefetchScalarGridSpec(
            num_scalar_prefetch=2,
            grid=(1,),
            in_specs=[
                pl.BlockSpec((2, owned, part, BLOCK), lambda i, w, c: (0, 0, w[1], 0)),
                whole(tokens.shape),
            ],
            out_specs=(whole((slots, part, BLOCK)), whole((my_blocks, tok_rows, BLOCK))),
        ),
        compiler_params=params,
        name="send_pack",
    )(where, tile_cols, tiles, tokens)

    def exchange(values):
        shape = (members, -1) + values.shape[1:]
        return lax.all_to_all(values.reshape(shape), "mp", 0, 0).reshape(values.shape)

    rows = [[x * ring + z for z in range(ring)] for x in range(sides)]

    def turn(value, s):
        pairs = [
            (x * ring + z, (x + s) % sides * ring + z) for x in range(sides) for z in range(ring)
        ]
        return lax.ppermute(value, "mp", pairs)

    def along(value, s):
        pairs = [
            (x * ring + z, x * ring + (z + s) % ring) for x in range(sides) for z in range(ring)
        ]
        return lax.ppermute(value, "mp", pairs)

    row_tok = jnp.stack([my_tok] + [along(my_tok, s) for s in range(1, ring)])
    table, count = slot_table(tile_rows, tile_cols, me, members, panels)
    incoming, row_tok = lax.optimization_barrier((exchange(outgoing), row_tok))
    ordered = pl.pallas_call(
        sort_kernel,
        out_shape=jax.ShapeDtypeStruct((used, part, BLOCK), BF16),
        grid_spec=pltpu.PrefetchScalarGridSpec(
            num_scalar_prefetch=1,
            grid=(1,),
            in_specs=[whole((slots, part, BLOCK))],
            out_specs=whole((used, part, BLOCK)),
        ),
        compiler_params=params,
        name="sort_slots",
    )(table, incoming)
    held = lax.all_gather(ordered, "dp")
    pieces = [row_tok] + [turn(row_tok, s) for s in range(1, sides)]

    per_panel = 2 * MOST
    hidden, grads, *terms = pl.pallas_call(
        lambda *refs: main_kernel(sides, *refs),
        out_shape=(
            jax.ShapeDtypeStruct(cotangent.shape, BF16),
            jax.ShapeDtypeStruct((groups, used, part, BLOCK), BF16),
        )
        + (jax.ShapeDtypeStruct((each, tok_rows, BLOCK), BF16),) * sides,
        grid_spec=pltpu.PrefetchScalarGridSpec(
            num_scalar_prefetch=3,
            grid=(panels,),
            in_specs=[pl.BlockSpec(memory_space=pl.ANY)] * sides
            + [
                pl.BlockSpec((groups, per_panel, part, BLOCK), lambda p, *_: (0, p, 0, 0)),
                pl.BlockSpec((tok_rows, BLOCK), lambda p, *_: (0, p)),
            ],
            out_specs=(
                pl.BlockSpec((tok_rows, BLOCK), lambda p, *_: (0, p)),
                pl.BlockSpec((groups, per_panel, part, BLOCK), lambda p, *_: (0, p, 0, 0)),
            )
            + (whole((each, tok_rows, BLOCK)),) * sides,
            scratch_shapes=[
                pltpu.VMEM((row_blocks, tok_rows, BLOCK), BF16),
                pltpu.VMEM((row_blocks, BLOCK, tok_rows), BF16),
                pltpu.VMEM((row_blocks, tok_rows, BLOCK), F32),
                pltpu.SemaphoreType.DMA((sides, ring)),
            ],
        ),
        compiler_params=params,
        name="gated_pair",
    )(table, count, where, *pieces, held, cotangent)

    my_grads = lax.psum_scatter(grads, "dp", scatter_dimension=0, tiled=False)
    arrived = [terms[0]] + [turn(terms[s], s) for s in range(1, sides)]
    row_terms = pl.pallas_call(
        add_kernel,
        out_shape=jax.ShapeDtypeStruct((each, tok_rows, BLOCK), BF16),
        compiler_params=params,
        name="row_sum",
    )(*arrived)
    my_grads, row_terms = lax.optimization_barrier((my_grads, row_terms))
    returning = pl.pallas_call(
        unsort_kernel,
        out_shape=jax.ShapeDtypeStruct((slots, part, BLOCK), BF16),
        grid_spec=pltpu.PrefetchScalarGridSpec(
            num_scalar_prefetch=2,
            grid=(1,),
            in_specs=[whole((used, part, BLOCK))],
            out_specs=whole((slots, part, BLOCK)),
        ),
        compiler_params=params,
        name="unsort_slots",
    )(table, count, my_grads)
    back = exchange(returning)
    own = pl.pallas_call(
        lambda *refs: own_kernel(panels, *refs),
        out_shape=jax.ShapeDtypeStruct((2, owned, part, BLOCK), BF16),
        grid_spec=pltpu.PrefetchScalarGridSpec(
            num_scalar_prefetch=2,
            grid=(1,),
            in_specs=[whole((slots, part, BLOCK))],
            out_specs=whole((2, owned, part, BLOCK)),
        ),
        compiler_params=params,
        name="own_slots",
    )(where, tile_cols, back)
    own, row_terms = lax.optimization_barrier((own, row_terms))
    full = lax.all_gather(own, "dp").reshape(groups, 2 * owned, part, BLOCK)
    column = lax.all_to_all(
        row_terms.reshape(ring, my_blocks, tok_rows, BLOCK), "mp", 0, 0, axis_index_groups=rows
    )
    input_grad = pl.pallas_call(
        sum_kernel,
        out_shape=jax.ShapeDtypeStruct(tokens.shape, BF16),
        compiler_params=params,
        name="input_sum",
    )(column)
    some = 2 * owned // 6
    tile_grads = pl.pallas_call(
        widen_kernel,
        out_shape=jax.ShapeDtypeStruct((2 * owned, BLOCK, BLOCK), F32),
        grid=(6,),
        in_specs=[pl.BlockSpec((groups, some, part, BLOCK), lambda i: (0, i, 0, 0))],
        out_specs=pl.BlockSpec((some, BLOCK, BLOCK), lambda i: (i, 0, 0)),
        compiler_params=params,
        name="widen",
    )(full).reshape(tiles.shape)
    return hidden, input_grad, tile_grads


def solution(mesh):
    in_specs = (P("dp", "mp"), P("dp", "mp"), P(None, "mp", None, None), P(), P())
    out_specs = (P("dp", "mp"), P("dp", "mp"), P(None, "mp", None, None))
    return jax.shard_map(
        per_device, mesh=mesh, in_specs=in_specs, out_specs=out_specs, check_vma=False
    )
```

```python
import jax
import jax.numpy as jnp
from jax import lax
from jax.experimental import pallas as pl
from jax.experimental.pallas import tpu as pltpu
from jax.sharding import PartitionSpec as P

BLOCK = 128
MOST = 12
PAIR = 3
GROUP = 4
F32 = jnp.float32
BF16 = jnp.bfloat16


def nt(a, b):
    return lax.dot_general(a, b, (((1,), (1,)), ((), ())), preferred_element_type=F32)


def nn(a, b):
    return lax.dot_general(a, b, (((1,), (0,)), ((), ())), preferred_element_type=F32)


def slot_table(tile_rows, tile_cols, me, members, panels):
    owned = tile_cols.shape[1] // members
    cols = tile_cols.reshape(2, members, owned)
    rows = tile_rows.reshape(2, members, owned)
    local = cols - me * panels
    holder = cols // panels
    pad = jnp.full((2, members, 2), -1, jnp.int32)

    def run(values):
        one = jnp.concatenate([pad[:, :, :1], values[:, :, :-1]], axis=2)
        two = jnp.concatenate([pad, values[:, :, :-2]], axis=2)
        return (values == one).astype(jnp.int32) + (values == two).astype(jnp.int32)

    rank = run(holder)
    within = run(cols)
    place = (
        jnp.arange(members)[None, :, None] * (2 * PAIR)
        + jnp.arange(2)[:, None, None] * PAIR
        + rank
    )
    value = place * 64 + rows
    mine = local[None] == jnp.arange(panels)[:, None, None, None]
    count = jnp.sum(mine.astype(jnp.int32), axis=3)
    before = jnp.arange(members)[:, None] > jnp.arange(members)[None, :]
    earlier = jnp.sum(jnp.where(before, count[:, :, None, :], 0), axis=3)
    place_in_panel = jnp.where(mine, earlier[..., None] + within[None], -1)
    hit = place_in_panel[:, :, None] == jnp.arange(MOST)[:, None, None]
    table = jnp.sum(jnp.where(hit, value[None, :, None], 0), axis=(3, 4))
    return table.reshape(-1), jnp.sum(count, axis=2).reshape(-1)


def slot_of(cols_ref, me, owned, panels, visit):
    for m in range(2):

        def step(k, carry):
            last, rank = carry
            holder = cols_ref[m, me * owned + k] // panels
            rank = jnp.where(holder == last, rank + 1, 0)
            visit(m, k, holder * (2 * PAIR) + m * PAIR + rank)
            return holder, rank

        lax.fori_loop(0, owned, step, (jnp.int32(-1), jnp.int32(0)), unroll=6)


def send_kernel(panels, place_ref, cols_ref, tiles_ref, tokens_ref, out_ref, blocks_ref):
    owned = tiles_ref.shape[1]

    def visit(m, k, slot):
        out_ref[slot] = tiles_ref[m, k]

    slot_of(cols_ref, place_ref[0], owned, panels, visit)
    for b in range(blocks_ref.shape[0]):
        blocks_ref[b] = tokens_ref[:, b * BLOCK : (b + 1) * BLOCK]


def own_kernel(panels, place_ref, cols_ref, back_ref, out_ref):
    owned = out_ref.shape[1]

    def visit(m, k, slot):
        out_ref[m, k] = back_ref[slot]

    slot_of(cols_ref, place_ref[0], owned, panels, visit)


def sort_kernel(table_ref, in_ref, out_ref):
    def step(s, carry):
        out_ref[s] = in_ref[table_ref[s] >> 6]
        return carry

    lax.fori_loop(0, out_ref.shape[0], step, 0, unroll=8)


def unsort_kernel(table_ref, count_ref, in_ref, out_ref):
    for q in range(in_ref.shape[0] // MOST):

        def step(t, carry):
            s = q * MOST + t
            out_ref[table_ref[s] >> 6] = in_ref[s]
            return carry

        lax.fori_loop(0, count_ref[q], step, 0)


def main_kernel(
    sides,
    ring,
    table_ref,
    count_ref,
    where_ref,
    *refs,
):
    pieces, refs = refs[: ring + 1], refs[ring + 1 :]
    tile_ref, cot_ref, hidden_ref, grad_ref, *refs = refs
    terms = refs[:sides]
    tok_ref, tok_t, total, sems = refs[sides:]
    p = pl.program_id(0)
    blocks = tok_ref.shape[0]
    each = blocks // sides
    side = where_ref[2]

    @pl.when(p == 0)
    def _():
        steps = [j for j in range(ring) if j != ring // 2]
        held = [(j, s, piece.at[s]) for j, piece in zip(steps, pieces) for s in range(sides)]
        held += [
            (ring // 2, k * sides // 2 + s, piece.at[s])
            for k, piece in enumerate(pieces[-2:])
            for s in range(sides // 2)
        ]
        copies = [
            pltpu.make_async_copy(
                piece,
                tok_ref.at[
                    pl.ds(
                        lax.rem(side + sides - s, sides) * each
                        + lax.rem(where_ref[3] + ring - j, ring) * (each // ring),
                        each // ring,
                    )
                ],
                sems.at[s, j],
            )
            for j, s, piece in held
        ]
        for copy in copies:
            copy.start()
        for copy in copies:
            copy.wait()

        def step(b, carry):
            tok_t[b] = tok_ref[b].T
            total[b] = jnp.zeros_like(total[b])
            return carry

        lax.fori_loop(0, blocks, step, 0)

    def work(counts):
        at = [
            [table_ref[(p * 2 + m) * MOST + t] & 63 for t in range(counts[m])] for m in range(2)
        ]

        def weights(m, first):
            return tile_ref[:, m * MOST + first : m * MOST + first + GROUP]

        def stacked(m, first):
            w = weights(m, first)
            return jnp.concatenate([w[:, i].reshape(BLOCK, BLOCK) for i in range(GROUP)], axis=0)

        pre = []
        for m in range(2):
            acc = None
            for first in range(0, counts[m], GROUP):
                lhs = jnp.concatenate([tok_ref[at[m][first + i]] for i in range(GROUP)], axis=1)
                term = nn(lhs, stacked(m, first))
                acc = term if acc is None else acc + term
            pre.append(acc)
        gate, up = pre
        sig = 1.0 / (1.0 + jnp.exp(-gate))
        hidden_ref[...] = (gate * sig * up).astype(BF16)
        cot = cot_ref[...].astype(F32)
        grads = (
            (cot * up * sig * (1.0 + gate * (1.0 - sig))).astype(BF16),
            (cot * gate * sig).astype(BF16),
        )
        for m in range(2):
            for first in range(0, counts[m], GROUP):
                lhs = jnp.concatenate([tok_t[at[m][first + i]] for i in range(GROUP)], axis=0)
                out = nn(lhs, grads[m]).astype(BF16)
                back = nt(grads[m], stacked(m, first))
                for i in range(GROUP):
                    part = out[i * BLOCK : (i + 1) * BLOCK]
                    grad_ref[:, m * MOST + first + i] = part.reshape(8, BLOCK // 8, BLOCK)
                    total[at[m][first + i]] += back[:, i * BLOCK : (i + 1) * BLOCK]

    many = [count_ref[p * 2 + m] > GROUP for m in range(2)]
    for most in range(4):
        picked = [bool(most & 1), bool(most & 2)]
        same = [many[m] if picked[m] else jnp.logical_not(many[m]) for m in range(2)]

        @pl.when(jnp.logical_and(same[0], same[1]))
        def _():
            work([MOST if picked[m] else GROUP for m in range(2)])

    @pl.when(p == pl.num_programs(0) - 1)
    def _():
        for s in range(sides):
            base = lax.rem(side + s, sides) * each

            def step(b, carry):
                terms[s][b] = total[base + b].astype(BF16)
                return carry

            lax.fori_loop(0, each, step, 0)


def sum_kernel(in_ref, out_ref):
    def step(k, acc):
        return tuple(a + in_ref[k, i].astype(F32) for i, a in enumerate(acc))

    count = in_ref.shape[1]
    acc = lax.fori_loop(
        0, in_ref.shape[0], step, tuple(jnp.zeros(in_ref.shape[2:], F32) for _ in range(count))
    )
    for i in range(count):
        out_ref[:, i * BLOCK : (i + 1) * BLOCK] = acc[i].astype(BF16)


def add_kernel(*refs):
    out_ref = refs[-1]

    def step(b, carry):
        out_ref[b] = sum(r[b].astype(F32) for r in refs[:-1]).astype(BF16)
        return carry

    lax.fori_loop(0, out_ref.shape[0], step, 0)


def widen_kernel(in_ref, out_ref):
    parts, count, part, _ = in_ref.shape

    def step(i, carry):
        out_ref[i] = in_ref[:, i].reshape(parts * part, BLOCK).astype(F32)
        return carry

    lax.fori_loop(0, count, step, 0, unroll=2)


def whole(shape):
    return pl.BlockSpec(shape, lambda *_: (0,) * len(shape))


def per_device(tokens, cotangent, tiles, tile_rows, tile_cols):
    groups = lax.axis_size("dp")
    members = lax.axis_size("mp")
    me = lax.axis_index("mp")
    mygroup = lax.axis_index("dp")
    owned = tiles.shape[1]
    tok_rows, my_features = tokens.shape
    my_blocks = my_features // BLOCK
    row_blocks = my_blocks * members
    panels = cotangent.shape[1] // BLOCK
    part = BLOCK // groups
    slots = members * 2 * PAIR
    used = panels * 2 * MOST
    params = pltpu.CompilerParams(vmem_limit_bytes=48 * 1024 * 1024)
    alone = pltpu.CompilerParams(vmem_limit_bytes=60 * 1024 * 1024)
    sides = 4
    ring = members // sides
    each = row_blocks // sides
    where = jnp.stack([me, mygroup, me // ring, me % ring]).astype(jnp.int32)

    outgoing, my_tok = pl.pallas_call(
        lambda *refs: send_kernel(panels, *refs),
        out_shape=(
            jax.ShapeDtypeStruct((slots, part, BLOCK), BF16),
            jax.ShapeDtypeStruct((my_blocks, tok_rows, BLOCK), BF16),
        ),
        grid_spec=pltpu.PrefetchScalarGridSpec(
            num_scalar_prefetch=2,
            grid=(1,),
            in_specs=[
                pl.BlockSpec((2, owned, part, BLOCK), lambda i, w, c: (0, 0, w[1], 0)),
                whole(tokens.shape),
            ],
            out_specs=(whole((slots, part, BLOCK)), whole((my_blocks, tok_rows, BLOCK))),
        ),
        compiler_params=alone,
        name="send_pack",
    )(where, tile_cols, tiles, tokens)

    def exchange(values):
        shape = (members, -1) + values.shape[1:]
        return lax.all_to_all(values.reshape(shape), "mp", 0, 0).reshape(values.shape)

    rows = [[x * ring + z for z in range(ring)] for x in range(sides)]

    def turn(value, s):
        pairs = [
            (x * ring + z, (x + s) % sides * ring + z) for x in range(sides) for z in range(ring)
        ]
        return lax.ppermute(value, "mp", pairs)

    def along(value, s):
        pairs = [
            (x * ring + z, x * ring + (z + s) % ring) for x in range(sides) for z in range(ring)
        ]
        return lax.ppermute(value, "mp", pairs)

    line_tok = jnp.stack([my_tok] + [turn(my_tok, s) for s in range(1, sides)])
    table, count = slot_table(tile_rows, tile_cols, me, members, panels)
    incoming, line_tok = lax.optimization_barrier((exchange(outgoing), line_tok))
    ordered = pl.pallas_call(
        sort_kernel,
        out_shape=jax.ShapeDtypeStruct((used, part, BLOCK), BF16),
        grid_spec=pltpu.PrefetchScalarGridSpec(
            num_scalar_prefetch=1,
            grid=(1,),
            in_specs=[whole((slots, part, BLOCK))],
            out_specs=whole((used, part, BLOCK)),
        ),
        compiler_params=params,
        name="sort_slots",
    )(table, incoming)
    held = lax.all_gather(ordered, "dp")
    ups, downs = [line_tok], [line_tok]
    for _ in range(ring // 2 - 1):
        ups.append(along(ups[-1], 1))
        downs.append(along(downs[-1], -1))
    far = [along(ups[-1][: sides // 2], 1), along(downs[-1][sides // 2 :], -1)]
    pieces = ups + downs[:0:-1] + far

    per_panel = 2 * MOST
    hidden, grads, *terms = pl.pallas_call(
        lambda *refs: main_kernel(sides, ring, *refs),
        out_shape=(
            jax.ShapeDtypeStruct(cotangent.shape, BF16),
            jax.ShapeDtypeStruct((groups, used, part, BLOCK), BF16),
        )
        + (jax.ShapeDtypeStruct((each, tok_rows, BLOCK), BF16),) * sides,
        grid_spec=pltpu.PrefetchScalarGridSpec(
            num_scalar_prefetch=3,
            grid=(panels,),
            in_specs=[pl.BlockSpec(memory_space=pl.ANY)] * len(pieces)
            + [
                pl.BlockSpec((groups, per_panel, part, BLOCK), lambda p, *_: (0, p, 0, 0)),
                pl.BlockSpec((tok_rows, BLOCK), lambda p, *_: (0, p)),
            ],
            out_specs=(
                pl.BlockSpec((tok_rows, BLOCK), lambda p, *_: (0, p)),
                pl.BlockSpec((groups, per_panel, part, BLOCK), lambda p, *_: (0, p, 0, 0)),
            )
            + (whole((each, tok_rows, BLOCK)),) * sides,
            scratch_shapes=[
                pltpu.VMEM((row_blocks, tok_rows, BLOCK), BF16),
                pltpu.VMEM((row_blocks, BLOCK, tok_rows), BF16),
                pltpu.VMEM((row_blocks, tok_rows, BLOCK), F32),
                pltpu.SemaphoreType.DMA((sides, ring)),
            ],
        ),
        compiler_params=alone,
        name="gated_pair",
    )(table, count, where, *pieces, held, cotangent)

    my_grads = lax.psum_scatter(grads, "dp", scatter_dimension=0, tiled=False)
    arrived = [terms[0]] + [turn(terms[s], s) for s in range(1, sides)]
    row_terms = pl.pallas_call(
        add_kernel,
        out_shape=jax.ShapeDtypeStruct((each, tok_rows, BLOCK), BF16),
        compiler_params=params,
        name="row_sum",
    )(*arrived)
    my_grads, row_terms = lax.optimization_barrier((my_grads, row_terms))
    returning = pl.pallas_call(
        unsort_kernel,
        out_shape=jax.ShapeDtypeStruct((slots, part, BLOCK), BF16),
        grid_spec=pltpu.PrefetchScalarGridSpec(
            num_scalar_prefetch=2,
            grid=(1,),
            in_specs=[whole((used, part, BLOCK))],
            out_specs=whole((slots, part, BLOCK)),
        ),
        compiler_params=params,
        name="unsort_slots",
    )(table, count, my_grads)
    back = exchange(returning)
    own = pl.pallas_call(
        lambda *refs: own_kernel(panels, *refs),
        out_shape=jax.ShapeDtypeStruct((2, owned, part, BLOCK), BF16),
        grid_spec=pltpu.PrefetchScalarGridSpec(
            num_scalar_prefetch=2,
            grid=(1,),
            in_specs=[whole((slots, part, BLOCK))],
            out_specs=whole((2, owned, part, BLOCK)),
        ),
        compiler_params=params,
        name="own_slots",
    )(where, tile_cols, back)
    own, row_terms = lax.optimization_barrier((own, row_terms))
    full = lax.all_gather(own, "dp").reshape(groups, 2 * owned, part, BLOCK)
    column = lax.all_to_all(
        row_terms.reshape(ring, my_blocks, tok_rows, BLOCK), "mp", 0, 0, axis_index_groups=rows
    )
    input_grad = pl.pallas_call(
        sum_kernel,
        out_shape=jax.ShapeDtypeStruct(tokens.shape, BF16),
        compiler_params=params,
        name="input_sum",
    )(column)
    some = 2 * owned // 6
    tile_grads = pl.pallas_call(
        widen_kernel,
        out_shape=jax.ShapeDtypeStruct((2 * owned, BLOCK, BLOCK), F32),
        grid=(6,),
        in_specs=[pl.BlockSpec((groups, some, part, BLOCK), lambda i: (0, i, 0, 0))],
        out_specs=pl.BlockSpec((some, BLOCK, BLOCK), lambda i: (i, 0, 0)),
        compiler_params=params,
        name="widen",
    )(full).reshape(tiles.shape)
    return hidden, input_grad, tile_grads


def solution(mesh):
    in_specs = (P("dp", "mp"), P("dp", "mp"), P(None, "mp", None, None), P(), P())
    out_specs = (P("dp", "mp"), P("dp", "mp"), P(None, "mp", None, None))
    return jax.shard_map(
        per_device, mesh=mesh, in_specs=in_specs, out_specs=out_specs, check_vma=False
    )
```

```python
import jax
import jax.numpy as jnp
from jax import lax
from jax.experimental import pallas as pl
from jax.experimental.pallas import tpu as pltpu
from jax.sharding import PartitionSpec as P

BLOCK = 128
MOST = 12
PAIR = 3
GROUP = 4
F32 = jnp.float32
BF16 = jnp.bfloat16


def nt(a, b):
    return lax.dot_general(a, b, (((1,), (1,)), ((), ())), preferred_element_type=F32)


def nn(a, b):
    return lax.dot_general(a, b, (((1,), (0,)), ((), ())), preferred_element_type=F32)


def slot_table(tile_rows, tile_cols, me, members, panels):
    owned = tile_cols.shape[1] // members
    cols = tile_cols.reshape(2, members, owned)
    rows = tile_rows.reshape(2, members, owned)
    local = cols - me * panels
    holder = cols // panels
    pad = jnp.full((2, members, 2), -1, jnp.int32)

    def run(values):
        one = jnp.concatenate([pad[:, :, :1], values[:, :, :-1]], axis=2)
        two = jnp.concatenate([pad, values[:, :, :-2]], axis=2)
        return (values == one).astype(jnp.int32) + (values == two).astype(jnp.int32)

    rank = run(holder)
    within = run(cols)
    value = jnp.arange(members)[None, :, None] * 256 + rank * 64 + rows
    mine = local[None] == jnp.arange(panels)[:, None, None, None]
    count = jnp.sum(mine.astype(jnp.int32), axis=3)
    before = jnp.arange(members)[:, None] > jnp.arange(members)[None, :]
    earlier = jnp.sum(jnp.where(before, count[:, :, None, :], 0), axis=3)
    place_in_panel = jnp.where(mine, earlier[..., None] + within[None], -1)
    hit = place_in_panel[:, :, None] == jnp.arange(MOST)[:, None, None]
    table = jnp.sum(jnp.where(hit, value[None, :, None], 0), axis=(3, 4))
    return jnp.swapaxes(table, 0, 1).reshape(-1), jnp.sum(count, axis=2).T.reshape(-1)


def slot_of(cols_ref, me, owned, panels, m, visit):
    def step(k, carry):
        last, rank = carry
        holder = cols_ref[m, me * owned + k] // panels
        rank = jnp.where(holder == last, rank + 1, 0)
        visit(k, holder, rank)
        return holder, rank

    lax.fori_loop(0, owned, step, (jnp.int32(-1), jnp.int32(0)), unroll=6)


def send_kernel(panels, place_ref, cols_ref, tiles_ref, tokens_ref, out_ref, blocks_ref):
    for m in range(2):

        def visit(k, holder, rank):
            out_ref[holder * (2 * PAIR) + m * PAIR + rank] = tiles_ref[m, k]

        slot_of(cols_ref, place_ref[0], tiles_ref.shape[1], panels, m, visit)
    for b in range(blocks_ref.shape[0]):
        blocks_ref[b] = tokens_ref[:, b * BLOCK : (b + 1) * BLOCK]


def own_kernel(panels, place_ref, cols_ref, back_ref, out_ref):
    for m in range(2):

        def visit(k, holder, rank):
            out_ref[m, k] = back_ref[holder * (2 * PAIR) + m * PAIR + rank]

        slot_of(cols_ref, place_ref[0], out_ref.shape[1], panels, m, visit)


def sort_kernel(table_ref, in_ref, out_ref):
    half = out_ref.shape[0] // 2
    for m in range(2):

        def step(s, carry):
            v = table_ref[m * half + s]
            out_ref[m * half + s] = in_ref[(v >> 8) * (2 * PAIR) + m * PAIR + ((v >> 6) & 3)]
            return carry

        lax.fori_loop(0, half, step, 0, unroll=6)


def unsort_kernel(table_ref, count_ref, *refs):
    out_ref = refs[-1]
    each = len(refs) // 2
    half = refs[0].shape[0]
    panels = half // MOST
    for m in range(2):
        in_refs = refs[m * each : (m + 1) * each]
        for q in range(panels):

            def step(g, carry):
                for i in range(GROUP):
                    s = q * MOST + g * GROUP + i
                    v = table_ref[m * half + s]
                    total = sum(r[s].astype(F32) for r in in_refs).astype(BF16)
                    out_ref[(v >> 8) * (2 * PAIR) + m * PAIR + ((v >> 6) & 3)] = total
                return carry

            lax.fori_loop(0, count_ref[m * panels + q] // GROUP, step, 0)


def core_kernel(where_ref, mine_ref, other_ref, *out_refs):
    for k, out_ref in enumerate(out_refs):
        y = lax.rem(where_ref[5] + k, 4)
        out_ref[...] = (mine_ref[y].astype(F32) + other_ref[y].astype(F32)).astype(BF16)


def main_kernel(sides, ring, panels, table_ref, count_ref, where_ref, *refs):
    pieces, refs = refs[: ring + 1], refs[ring + 1 :]
    tile_hbm, cot_ref, hidden_ref, *refs = refs
    grads_hbm, refs = (refs[:2], refs[2:4]), refs[4:]
    terms_ref, tok_ref, tok_t, total, tile_ref, grad_ref, pair_ref, *refs = refs
    tok_sems, in_sems, out_sems = refs
    blocks = tok_ref.shape[0]
    each = blocks // sides
    turned = -(-blocks // panels)
    side = where_ref[2]

    core = where_ref[4]

    def loads(p):
        for m in range(2):
            at = pl.ds((m * panels + p) * MOST, MOST)
            yield pltpu.make_async_copy(tile_hbm.at[:, at], tile_ref.at[:, at], in_sems.at[m, p])

    def stores(p):
        for m in range(2):
            at, to = pl.ds((m * panels + p) * MOST, MOST), pl.ds(p * MOST, MOST)
            for k in range(2):
                yield pltpu.make_async_copy(
                    grad_ref.at[k, :, at], grads_hbm[k][m].at[:, to], out_sems.at[k, m, p]
                )

    steps = [j for j in range(ring) if j != ring // 2]
    held = [(j, s, piece.at[s]) for j, piece in zip(steps, pieces) for s in range(sides)]
    held += [
        (ring // 2, k * sides // 2 + s, piece.at[s])
        for k, piece in enumerate(pieces[-2:])
        for s in range(sides // 2)
    ]
    copies = [
        pltpu.make_async_copy(
            piece,
            tok_ref.at[
                pl.ds(
                    lax.rem(side + sides - s, sides) * each
                    + lax.rem(where_ref[3] + ring - j, ring) * (each // ring),
                    each // ring,
                )
            ],
            tok_sems.at[s, j],
        )
        for j, s, piece in held
    ]
    for copy in copies:
        copy.start()
    for p in range(panels):
        for copy in loads(p):
            copy.start()

    def clear(b, carry):
        total[b] = jnp.zeros_like(total[b])
        return carry

    lax.fori_loop(0, blocks, clear, 0)
    for copy in copies:
        copy.wait()

    def stacked(p, m, first):
        w = tile_ref[:, pl.ds((m * panels + p) * MOST + first, GROUP)]
        return jnp.concatenate([w[:, i].reshape(BLOCK, BLOCK) for i in range(GROUP)], axis=0)

    def by_counts(p, work):
        many = [count_ref[m * panels + p] > GROUP for m in range(2)]
        for most in range(4):
            picked = [bool(most & 1), bool(most & 2)]
            same = [many[m] if picked[m] else jnp.logical_not(many[m]) for m in range(2)]

            @pl.when(jnp.logical_and(same[0], same[1]))
            def _():
                counts = [MOST if picked[m] else GROUP for m in range(2)]
                at = [
                    [table_ref[(m * panels + p) * MOST + t] & 63 for t in range(counts[m])]
                    for m in range(2)
                ]
                work(p, counts, at)

    def forward(p, counts, at):
        for i in range(turned):
            b = jnp.minimum(p * turned + i, blocks - 1)
            tok_t[b] = tok_ref[b].T
        pre = []
        for m in range(2):
            acc = None
            for first in range(0, counts[m], GROUP):
                lhs = jnp.concatenate([tok_ref[at[m][first + i]] for i in range(GROUP)], axis=1)
                term = nn(lhs, stacked(p, m, first))
                acc = term if acc is None else acc + term
            pre.append(acc)
        gate, up = pre
        sig = 1.0 / (1.0 + jnp.exp(-gate))
        columns = pl.ds(pl.multiple_of(p * BLOCK, BLOCK), BLOCK)
        hidden_ref[:, columns] = (gate * sig * up).astype(BF16)
        cot = cot_ref[:, columns].astype(F32)
        pair_ref[p * 2] = (cot * up * sig * (1.0 + gate * (1.0 - sig))).astype(BF16)
        pair_ref[p * 2 + 1] = (cot * gate * sig).astype(BF16)

    def backward(p, counts, at):
        for m in range(2):
            grad = pair_ref[p * 2 + m]
            for first in range(0, counts[m], GROUP):
                lhs = jnp.concatenate([tok_t[at[m][first + i]] for i in range(GROUP)], axis=0)
                out = nn(lhs, grad).astype(BF16)
                back = nt(grad, stacked(p, m, first))
                for i in range(GROUP):
                    part = out[i * BLOCK : (i + 1) * BLOCK].reshape(4, 2, BLOCK // 8, BLOCK)
                    slot = (m * panels + p) * MOST + first + i
                    grad_ref[core, :, slot] = part[:, 0]
                    grad_ref[1 - core, :, slot] = part[:, 1]
                    total[at[m][first + i]] += back[:, i * BLOCK : (i + 1) * BLOCK]

    def first_pass(p, carry):
        for copy in loads(p):
            copy.wait()
        by_counts(p, forward)
        return carry

    def second_pass(p, carry):
        by_counts(p, backward)
        for copy in stores(p):
            copy.start()
        return carry

    lax.fori_loop(0, panels, first_pass, 0)
    lax.fori_loop(0, panels, second_pass, 0)

    def step(b, carry):
        terms_ref[b] = total[b].astype(BF16)
        return carry

    lax.fori_loop(0, blocks, step, 0, unroll=2)
    for p in range(panels):
        for copy in stores(p):
            copy.wait()


def sum_kernel(in_ref, out_ref):
    def step(k, acc):
        return tuple(a + in_ref[k, i].astype(F32) for i, a in enumerate(acc))

    count = in_ref.shape[1]
    acc = lax.fori_loop(
        0, in_ref.shape[0], step, tuple(jnp.zeros(in_ref.shape[2:], F32) for _ in range(count))
    )
    for i in range(count):
        out_ref[:, i * BLOCK : (i + 1) * BLOCK] = acc[i].astype(BF16)


def widen_kernel(in_ref, out_ref):
    parts, count, part, _ = in_ref.shape

    def step(i, carry):
        out_ref[i] = in_ref[:, i].reshape(parts * part, BLOCK).astype(F32)
        return carry

    lax.fori_loop(0, count, step, 0, unroll=2)


def whole(shape):
    return pl.BlockSpec(shape, lambda *_: (0,) * len(shape))


def per_device(tokens, cotangent, tiles, tile_rows, tile_cols):
    groups = lax.axis_size("dp")
    members = lax.axis_size("mp")
    me = lax.axis_index("mp")
    mygroup = lax.axis_index("dp")
    owned = tiles.shape[1]
    tok_rows, my_features = tokens.shape
    my_blocks = my_features // BLOCK
    row_blocks = my_blocks * members
    panels = cotangent.shape[1] // BLOCK
    part = BLOCK // groups
    slots = members * 2 * PAIR
    used = panels * 2 * MOST
    params = pltpu.CompilerParams(vmem_limit_bytes=48 * 1024 * 1024)
    alone = pltpu.CompilerParams(vmem_limit_bytes=60 * 1024 * 1024)
    sides = 4
    ring = members // sides
    each = row_blocks // sides
    where = jnp.stack([me, mygroup, me // ring, me % ring, mygroup % 2, mygroup // 2]).astype(jnp.int32)

    outgoing, my_tok = pl.pallas_call(
        lambda *refs: send_kernel(panels, *refs),
        out_shape=(
            jax.ShapeDtypeStruct((slots, part, BLOCK), BF16),
            jax.ShapeDtypeStruct((my_blocks, tok_rows, BLOCK), BF16),
        ),
        grid_spec=pltpu.PrefetchScalarGridSpec(
            num_scalar_prefetch=2,
            grid=(1,),
            in_specs=[
                pl.BlockSpec((2, owned, part, BLOCK), lambda i, w, c: (0, 0, w[1], 0)),
                whole(tokens.shape),
            ],
            out_specs=(whole((slots, part, BLOCK)), whole((my_blocks, tok_rows, BLOCK))),
        ),
        compiler_params=alone,
        name="send_pack",
    )(where, tile_cols, tiles, tokens)

    def exchange(values):
        shape = (members, -1) + values.shape[1:]
        return lax.all_to_all(values.reshape(shape), "mp", 0, 0).reshape(values.shape)

    rows = [[x * ring + z for z in range(ring)] for x in range(sides)]

    def turn(value, s):
        pairs = [
            (x * ring + z, (x + s) % sides * ring + z) for x in range(sides) for z in range(ring)
        ]
        return lax.ppermute(value, "mp", pairs)

    def along(value, s):
        pairs = [
            (x * ring + z, x * ring + (z + s) % ring) for x in range(sides) for z in range(ring)
        ]
        return lax.ppermute(value, "mp", pairs)

    line_tok = jnp.stack([my_tok] + [turn(my_tok, s) for s in range(1, sides)])
    table, count = slot_table(tile_rows, tile_cols, me, members, panels)
    incoming, line_tok = lax.optimization_barrier((exchange(outgoing), line_tok))
    ordered = pl.pallas_call(
        sort_kernel,
        out_shape=jax.ShapeDtypeStruct((used, part, BLOCK), BF16),
        grid_spec=pltpu.PrefetchScalarGridSpec(
            num_scalar_prefetch=1,
            grid=(1,),
            in_specs=[whole((slots, part, BLOCK))],
            out_specs=whole((used, part, BLOCK)),
        ),
        compiler_params=params,
        name="sort_slots",
    )(table, incoming)
    held = lax.all_gather(ordered, "dp")
    ups, downs = [line_tok], [line_tok]
    for _ in range(ring // 2 - 1):
        ups.append(along(ups[-1], 1))
        downs.append(along(downs[-1], -1))
    far = [along(ups[-1][: sides // 2], 1), along(downs[-1][sides // 2 :], -1)]
    pieces = ups + downs[:0:-1] + far

    anywhere = pl.BlockSpec(memory_space=pl.ANY)
    split = jax.ShapeDtypeStruct((4, used // 2, part, BLOCK), BF16)
    hidden, mine_g, mine_u, other_g, other_u, terms = pl.pallas_call(
        lambda *refs: main_kernel(sides, ring, panels, *refs),
        out_shape=(
            jax.ShapeDtypeStruct(cotangent.shape, BF16),
            *(split,) * 4,
        )
        + (jax.ShapeDtypeStruct((row_blocks, tok_rows, BLOCK), BF16),),
        grid_spec=pltpu.PrefetchScalarGridSpec(
            num_scalar_prefetch=3,
            grid=(1,),
            in_specs=[anywhere] * (len(pieces) + 1) + [whole(cotangent.shape)],
            out_specs=(whole(cotangent.shape), *(anywhere,) * 4)
            + (whole((row_blocks, tok_rows, BLOCK)),),
            scratch_shapes=[
                pltpu.VMEM((row_blocks, tok_rows, BLOCK), BF16),
                pltpu.VMEM((row_blocks, BLOCK, tok_rows), BF16),
                pltpu.VMEM((row_blocks, tok_rows, BLOCK), F32),
                pltpu.VMEM((groups, used, part, BLOCK), BF16),
                pltpu.VMEM((2, 4, used, part, BLOCK), BF16),
                pltpu.VMEM((2 * panels, tok_rows, BLOCK), BF16),
                pltpu.SemaphoreType.DMA((sides, ring)),
                pltpu.SemaphoreType.DMA((2, panels)),
                pltpu.SemaphoreType.DMA((2, 2, panels)),
            ],
        ),
        compiler_params=alone,
        name="gated_pair",
    )(table, count, where, *pieces, held, cotangent)

    def around(value, s):
        pairs = [(y * 2 + c, (y + s) % 4 * 2 + c) for y in range(4) for c in range(2)]
        return lax.ppermute(value, "dp", pairs)

    piece = jax.ShapeDtypeStruct((used // 2, part, BLOCK), BF16)

    def reduced(mine, other):
        block = pl.BlockSpec((4, MOST, part, BLOCK), lambda i, w: (0, i, 0, 0))
        return pl.pallas_call(
            core_kernel,
            out_shape=(piece,) * 4,
            grid_spec=pltpu.PrefetchScalarGridSpec(
                num_scalar_prefetch=1,
                grid=(panels,),
                in_specs=[block] * 2,
                out_specs=(pl.BlockSpec((MOST, part, BLOCK), lambda i, w: (i, 0, 0)),) * 4,
            ),
            compiler_params=params,
            name="core_sum",
        )(where, mine, other)

    mine = [mine_g, mine_u]
    other = [lax.ppermute(v, "dp", [(d, d ^ 1) for d in range(groups)]) for v in (other_g, other_u)]
    sent = [reduced(mine[m], other[m]) for m in range(2)]
    came = [[sent[m][0]] + [around(sent[m][s], s) for s in (1, 2, 3)] for m in range(2)]
    columns = [[x * ring + z for x in range(sides)] for z in range(ring)]
    row_terms = lax.psum_scatter(
        terms, "mp", scatter_dimension=0, axis_index_groups=columns, tiled=True
    )
    returning = pl.pallas_call(
        unsort_kernel,
        out_shape=jax.ShapeDtypeStruct((slots, part, BLOCK), BF16),
        grid_spec=pltpu.PrefetchScalarGridSpec(
            num_scalar_prefetch=2,
            grid=(1,),
            in_specs=[whole(piece.shape)] * 8,
            out_specs=whole((slots, part, BLOCK)),
        ),
        compiler_params=params,
        name="unsort_slots",
    )(table, count, *came[0], *came[1])
    own = pl.pallas_call(
        lambda *refs: own_kernel(panels, *refs),
        out_shape=jax.ShapeDtypeStruct((2, owned, part, BLOCK), BF16),
        grid_spec=pltpu.PrefetchScalarGridSpec(
            num_scalar_prefetch=2,
            grid=(1,),
            in_specs=[whole((slots, part, BLOCK))],
            out_specs=whole((2, owned, part, BLOCK)),
        ),
        compiler_params=params,
        name="own_slots",
    )(where, tile_cols, exchange(returning))
    own, row_terms = lax.optimization_barrier((own, row_terms))
    full = lax.all_gather(own, "dp").reshape(groups, 2 * owned, part, BLOCK)
    column = lax.all_to_all(
        row_terms.reshape(ring, my_blocks, tok_rows, BLOCK), "mp", 0, 0, axis_index_groups=rows
    )
    input_grad = pl.pallas_call(
        sum_kernel,
        out_shape=jax.ShapeDtypeStruct(tokens.shape, BF16),
        compiler_params=params,
        name="input_sum",
    )(column)
    some = 2 * owned // 6
    tile_grads = pl.pallas_call(
        widen_kernel,
        out_shape=jax.ShapeDtypeStruct((2 * owned, BLOCK, BLOCK), F32),
        grid=(6,),
        in_specs=[pl.BlockSpec((groups, some, part, BLOCK), lambda i: (0, i, 0, 0))],
        out_specs=pl.BlockSpec((some, BLOCK, BLOCK), lambda i: (i, 0, 0)),
        compiler_params=params,
        name="widen",
    )(full).reshape(tiles.shape)
    return hidden, input_grad, tile_grads


def solution(mesh):
    in_specs = (P("dp", "mp"), P("dp", "mp"), P(None, "mp", None, None), P(), P())
    out_specs = (P("dp", "mp"), P("dp", "mp"), P(None, "mp", None, None))
    return jax.shard_map(
        per_device, mesh=mesh, in_specs=in_specs, out_specs=out_specs, check_vma=False
    )
```

```python
import jax
import jax.numpy as jnp
from jax import lax
from jax.experimental import pallas as pl
from jax.experimental.pallas import tpu as pltpu
from jax.sharding import PartitionSpec as P

BLOCK = 128
MOST = 12
PAIR = 3
GROUP = 4
F32 = jnp.float32
BF16 = jnp.bfloat16


def nt(a, b):
    return lax.dot_general(a, b, (((1,), (1,)), ((), ())), preferred_element_type=F32)


def nn(a, b):
    return lax.dot_general(a, b, (((1,), (0,)), ((), ())), preferred_element_type=F32)


def slot_table(tile_rows, tile_cols, me, members, panels):
    owned = tile_cols.shape[1] // members
    cols = tile_cols.reshape(2, members, owned)
    rows = tile_rows.reshape(2, members, owned)
    local = cols - me * panels
    holder = cols // panels
    pad = jnp.full((2, members, 2), -1, jnp.int32)

    def run(values):
        one = jnp.concatenate([pad[:, :, :1], values[:, :, :-1]], axis=2)
        two = jnp.concatenate([pad, values[:, :, :-2]], axis=2)
        return (values == one).astype(jnp.int32) + (values == two).astype(jnp.int32)

    rank = run(holder)
    within = run(cols)
    value = jnp.arange(members)[None, :, None] * 256 + rank * 64 + rows
    mine = local[None] == jnp.arange(panels)[:, None, None, None]
    count = jnp.sum(mine.astype(jnp.int32), axis=3)
    before = jnp.arange(members)[:, None] > jnp.arange(members)[None, :]
    earlier = jnp.sum(jnp.where(before, count[:, :, None, :], 0), axis=3)
    place_in_panel = jnp.where(mine, earlier[..., None] + within[None], -1)
    hit = place_in_panel[:, :, None] == jnp.arange(MOST)[:, None, None]
    table = jnp.sum(jnp.where(hit, value[None, :, None], 0), axis=(3, 4))
    return jnp.swapaxes(table, 0, 1).reshape(-1), jnp.sum(count, axis=2).T.reshape(-1)


def slot_of(cols_ref, me, owned, panels, m, visit):
    by = 65536 // panels + 1

    def step(k, carry):
        last, rank = carry
        holder = (cols_ref[m, me * owned + k] * by) >> 16
        rank = jnp.where(holder == last, rank + 1, 0)
        visit(k, holder, rank)
        return holder, rank

    lax.fori_loop(0, owned, step, (jnp.int32(-1), jnp.int32(0)), unroll=7)


def send_kernel(panels, place_ref, cols_ref, tiles_ref, tokens_ref, out_ref, blocks_ref):
    for m in range(2):

        def visit(k, holder, rank):
            out_ref[holder * (2 * PAIR) + m * PAIR + rank] = tiles_ref[m, k]

        slot_of(cols_ref, place_ref[0], tiles_ref.shape[1], panels, m, visit)
    for b in range(blocks_ref.shape[0]):
        blocks_ref[b] = tokens_ref[:, b * BLOCK : (b + 1) * BLOCK]


def own_kernel(panels, place_ref, cols_ref, back_ref, out_ref):
    for m in range(2):

        def visit(k, holder, rank):
            out_ref[m, k] = back_ref[holder * (2 * PAIR) + m * PAIR + rank]

        slot_of(cols_ref, place_ref[0], out_ref.shape[1], panels, m, visit)


def sort_kernel(table_ref, in_ref, out_ref):
    half = out_ref.shape[0] // 2
    for m in range(2):

        def step(s, carry):
            v = table_ref[m * half + s]
            out_ref[m * half + s] = in_ref[(v >> 8) * (2 * PAIR) + m * PAIR + ((v >> 6) & 3)]
            return carry

        lax.fori_loop(0, half, step, 0, unroll=6)


def unsort_kernel(table_ref, count_ref, *refs):
    out_ref = refs[-1]
    each = len(refs) // 2
    half = refs[0].shape[0]
    panels = half // MOST
    for m in range(2):
        in_refs = refs[m * each : (m + 1) * each]
        for q in range(panels):

            def step(g, carry):
                for i in range(GROUP):
                    s = q * MOST + g * GROUP + i
                    v = table_ref[m * half + s]
                    total = sum(r[s].astype(F32) for r in in_refs).astype(BF16)
                    out_ref[(v >> 8) * (2 * PAIR) + m * PAIR + ((v >> 6) & 3)] = total
                return carry

            lax.fori_loop(0, count_ref[m * panels + q] // GROUP, step, 0)


def core_kernel(where_ref, mine_ref, other_ref, *out_refs):
    for k, out_ref in enumerate(out_refs):
        y = lax.rem(where_ref[5] + k, 4)
        out_ref[...] = (mine_ref[y].astype(F32) + other_ref[y].astype(F32)).astype(BF16)


def main_kernel(sides, ring, panels, table_ref, count_ref, where_ref, *refs):
    pieces, refs = refs[: ring + 1], refs[ring + 1 :]
    tile_hbm, cot_ref, hidden_ref, *refs = refs
    grads_hbm, refs = (refs[:2], refs[2:4]), refs[4:]
    terms_ref, tok_ref, tok_t, total, tile_ref, grad_ref, pair_ref, *refs = refs
    tok_sems, in_sems, out_sems = refs
    blocks = tok_ref.shape[0]
    each = blocks // sides
    turned = -(-blocks // panels)
    side = where_ref[2]

    core = where_ref[4]

    def loads(p):
        for m in range(2):
            at = pl.ds((m * panels + p) * MOST, MOST)
            yield pltpu.make_async_copy(tile_hbm.at[:, at], tile_ref.at[:, at], in_sems.at[m, p])

    def stores(p):
        for m in range(2):
            at, to = pl.ds((m * panels + p) * MOST, MOST), pl.ds(p * MOST, MOST)
            for k in range(2):
                yield pltpu.make_async_copy(
                    grad_ref.at[k, :, at], grads_hbm[k][m].at[:, to], out_sems.at[k, m, p]
                )

    steps = [j for j in range(ring) if j != ring // 2]
    held = [(j, s, piece.at[s]) for j, piece in zip(steps, pieces) for s in range(sides)]
    held += [
        (ring // 2, k * sides // 2 + s, piece.at[s])
        for k, piece in enumerate(pieces[-2:])
        for s in range(sides // 2)
    ]
    copies = [
        pltpu.make_async_copy(
            piece,
            tok_ref.at[
                pl.ds(
                    lax.rem(side + sides - s, sides) * each
                    + lax.rem(where_ref[3] + ring - j, ring) * (each // ring),
                    each // ring,
                )
            ],
            tok_sems.at[s, j],
        )
        for j, s, piece in held
    ]
    for copy in copies:
        copy.start()
    for p in range(panels):
        for copy in loads(p):
            copy.start()

    def clear(b, carry):
        total[b] = jnp.zeros_like(total[b])
        return carry

    lax.fori_loop(0, blocks, clear, 0)
    for copy in copies:
        copy.wait()

    def stacked(p, m, first):
        w = tile_ref[:, pl.ds((m * panels + p) * MOST + first, GROUP)]
        return jnp.concatenate([w[:, i].reshape(BLOCK, BLOCK) for i in range(GROUP)], axis=0)

    def by_counts(p, work):
        many = [count_ref[m * panels + p] > GROUP for m in range(2)]
        for most in range(4):
            picked = [bool(most & 1), bool(most & 2)]
            same = [many[m] if picked[m] else jnp.logical_not(many[m]) for m in range(2)]

            @pl.when(jnp.logical_and(same[0], same[1]))
            def _():
                counts = [MOST if picked[m] else GROUP for m in range(2)]
                at = [
                    [table_ref[(m * panels + p) * MOST + t] & 63 for t in range(counts[m])]
                    for m in range(2)
                ]
                work(p, counts, at)

    def forward(p, counts, at):
        for i in range(turned):
            b = jnp.minimum(p * turned + i, blocks - 1)
            tok_t[b] = tok_ref[b].T
        pre = []
        for m in range(2):
            acc = None
            for first in range(0, counts[m], GROUP):
                lhs = jnp.concatenate([tok_ref[at[m][first + i]] for i in range(GROUP)], axis=1)
                term = nn(lhs, stacked(p, m, first))
                acc = term if acc is None else acc + term
            pre.append(acc)
        gate, up = pre
        sig = 1.0 / (1.0 + jnp.exp(-gate))
        columns = pl.ds(pl.multiple_of(p * BLOCK, BLOCK), BLOCK)
        hidden_ref[:, columns] = (gate * sig * up).astype(BF16)
        cot = cot_ref[:, columns].astype(F32)
        pair_ref[p * 2] = (cot * up * sig * (1.0 + gate * (1.0 - sig))).astype(BF16)
        pair_ref[p * 2 + 1] = (cot * gate * sig).astype(BF16)

    def backward(p, counts, at):
        for m in range(2):
            grad = pair_ref[p * 2 + m]
            for first in range(0, counts[m], GROUP):
                lhs = jnp.concatenate([tok_t[at[m][first + i]] for i in range(GROUP)], axis=0)
                out = nn(lhs, grad).astype(BF16)
                back = nt(grad, stacked(p, m, first))
                for i in range(GROUP):
                    part = out[i * BLOCK : (i + 1) * BLOCK].reshape(4, 2, BLOCK // 8, BLOCK)
                    slot = (m * panels + p) * MOST + first + i
                    grad_ref[core, :, slot] = part[:, 0]
                    grad_ref[1 - core, :, slot] = part[:, 1]
                    total[at[m][first + i]] += back[:, i * BLOCK : (i + 1) * BLOCK]

    def first_pass(p, carry):
        for copy in loads(p):
            copy.wait()
        by_counts(p, forward)
        return carry

    def second_pass(p, carry):
        by_counts(p, backward)
        for copy in stores(p):
            copy.start()
        return carry

    lax.fori_loop(0, panels, first_pass, 0)
    lax.fori_loop(0, panels, second_pass, 0)

    def step(b, carry):
        terms_ref[b] = total[b].astype(BF16)
        return carry

    lax.fori_loop(0, blocks, step, 0, unroll=2)
    for p in range(panels):
        for copy in stores(p):
            copy.wait()


def widen_kernel(where_ref, *refs):
    pieces, (blocks_ref, out_hbm, flat_ref, in_ref, out_ref, in_sems, out_sems) = refs[:-7], refs[-7:]
    parts, count, part, _ = in_ref.shape
    cuts = in_sems.shape[1]
    stores = out_sems.shape[0]
    core, y = where_ref[4], where_ref[5]

    def load(i, h):
        chunk = lax.rem(y + 4 - i // 2, 4) * 2 + (1 - core if i % 2 else core)
        at = pl.ds(h * (count // cuts), count // cuts)
        return pltpu.make_async_copy(pieces[i].at[at], in_ref.at[chunk, at], in_sems.at[i, h])

    def store(i):
        at = pl.ds(i * (count // stores), count // stores)
        return pltpu.make_async_copy(out_ref.at[at], out_hbm.at[at], out_sems.at[i])

    for h in range(cuts):
        for i in range(parts):
            load(i, h).start()
    for b in range(blocks_ref.shape[0]):
        flat_ref[:, b * BLOCK : (b + 1) * BLOCK] = blocks_ref[b]
    for i in range(stores):
        if i % (stores // cuts) == 0:
            for k in range(parts):
                load(k, i // (stores // cuts)).wait()

        def step(k, carry):
            out_ref[k] = in_ref[:, k].reshape(parts * part, BLOCK).astype(F32)
            return carry

        lax.fori_loop(i * (count // stores), (i + 1) * (count // stores), step, 0, unroll=2)
        store(i).start()
    for i in range(stores):
        store(i).wait()


def whole(shape):
    return pl.BlockSpec(shape, lambda *_: (0,) * len(shape))


def per_device(tokens, cotangent, tiles, tile_rows, tile_cols):
    groups = lax.axis_size("dp")
    members = lax.axis_size("mp")
    me = lax.axis_index("mp")
    mygroup = lax.axis_index("dp")
    owned = tiles.shape[1]
    tok_rows, my_features = tokens.shape
    my_blocks = my_features // BLOCK
    row_blocks = my_blocks * members
    panels = cotangent.shape[1] // BLOCK
    part = BLOCK // groups
    slots = members * 2 * PAIR
    used = panels * 2 * MOST
    params = pltpu.CompilerParams(vmem_limit_bytes=48 * 1024 * 1024)
    alone = pltpu.CompilerParams(vmem_limit_bytes=60 * 1024 * 1024)
    sides = 4
    ring = members // sides
    each = row_blocks // sides
    where = jnp.stack([me, mygroup, me // ring, me % ring, mygroup % 2, mygroup // 2]).astype(jnp.int32)

    outgoing, my_tok = pl.pallas_call(
        lambda *refs: send_kernel(panels, *refs),
        out_shape=(
            jax.ShapeDtypeStruct((slots, part, BLOCK), BF16),
            jax.ShapeDtypeStruct((my_blocks, tok_rows, BLOCK), BF16),
        ),
        grid_spec=pltpu.PrefetchScalarGridSpec(
            num_scalar_prefetch=2,
            grid=(1,),
            in_specs=[
                pl.BlockSpec((2, owned, part, BLOCK), lambda i, w, c: (0, 0, w[1], 0)),
                whole(tokens.shape),
            ],
            out_specs=(whole((slots, part, BLOCK)), whole((my_blocks, tok_rows, BLOCK))),
        ),
        compiler_params=alone,
        name="send_pack",
    )(where, tile_cols, tiles, tokens)

    def exchange(values):
        shape = (members, -1) + values.shape[1:]
        return lax.all_to_all(values.reshape(shape), "mp", 0, 0).reshape(values.shape)

    rows = [[x * ring + z for z in range(ring)] for x in range(sides)]

    def turn(value, s):
        pairs = [
            (x * ring + z, (x + s) % sides * ring + z) for x in range(sides) for z in range(ring)
        ]
        return lax.ppermute(value, "mp", pairs)

    def along(value, s):
        pairs = [
            (x * ring + z, x * ring + (z + s) % ring) for x in range(sides) for z in range(ring)
        ]
        return lax.ppermute(value, "mp", pairs)

    line_tok = jnp.stack([my_tok] + [turn(my_tok, s) for s in range(1, sides)])
    table, count = slot_table(tile_rows, tile_cols, me, members, panels)
    incoming, line_tok = lax.optimization_barrier((exchange(outgoing), line_tok))
    ordered = pl.pallas_call(
        sort_kernel,
        out_shape=jax.ShapeDtypeStruct((used, part, BLOCK), BF16),
        grid_spec=pltpu.PrefetchScalarGridSpec(
            num_scalar_prefetch=1,
            grid=(1,),
            in_specs=[whole((slots, part, BLOCK))],
            out_specs=whole((used, part, BLOCK)),
        ),
        compiler_params=params,
        name="sort_slots",
    )(table, incoming)
    held = lax.all_gather(ordered, "dp")
    ups, downs = [line_tok], [line_tok]
    for _ in range(ring // 2 - 1):
        ups.append(along(ups[-1], 1))
        downs.append(along(downs[-1], -1))
    far = [along(ups[-1][: sides // 2], 1), along(downs[-1][sides // 2 :], -1)]
    pieces = ups + downs[:0:-1] + far

    anywhere = pl.BlockSpec(memory_space=pl.ANY)
    split = jax.ShapeDtypeStruct((4, used // 2, part, BLOCK), BF16)
    hidden, mine_g, mine_u, other_g, other_u, terms = pl.pallas_call(
        lambda *refs: main_kernel(sides, ring, panels, *refs),
        out_shape=(
            jax.ShapeDtypeStruct(cotangent.shape, BF16),
            *(split,) * 4,
        )
        + (jax.ShapeDtypeStruct((row_blocks, tok_rows, BLOCK), BF16),),
        grid_spec=pltpu.PrefetchScalarGridSpec(
            num_scalar_prefetch=3,
            grid=(1,),
            in_specs=[anywhere] * (len(pieces) + 1) + [whole(cotangent.shape)],
            out_specs=(whole(cotangent.shape), *(anywhere,) * 4)
            + (whole((row_blocks, tok_rows, BLOCK)),),
            scratch_shapes=[
                pltpu.VMEM((row_blocks, tok_rows, BLOCK), BF16),
                pltpu.VMEM((row_blocks, BLOCK, tok_rows), BF16),
                pltpu.VMEM((row_blocks, tok_rows, BLOCK), F32),
                pltpu.VMEM((groups, used, part, BLOCK), BF16),
                pltpu.VMEM((2, 4, used, part, BLOCK), BF16),
                pltpu.VMEM((2 * panels, tok_rows, BLOCK), BF16),
                pltpu.SemaphoreType.DMA((sides, ring)),
                pltpu.SemaphoreType.DMA((2, panels)),
                pltpu.SemaphoreType.DMA((2, 2, panels)),
            ],
        ),
        compiler_params=alone,
        name="gated_pair",
    )(table, count, where, *pieces, held, cotangent)

    def around(value, s):
        pairs = [(y * 2 + c, (y + s) % 4 * 2 + c) for y in range(4) for c in range(2)]
        return lax.ppermute(value, "dp", pairs)

    piece = jax.ShapeDtypeStruct((used // 2, part, BLOCK), BF16)

    def reduced(mine, other):
        block = pl.BlockSpec((4, MOST, part, BLOCK), lambda i, w: (0, i, 0, 0))
        return pl.pallas_call(
            core_kernel,
            out_shape=(piece,) * 4,
            grid_spec=pltpu.PrefetchScalarGridSpec(
                num_scalar_prefetch=1,
                grid=(panels,),
                in_specs=[block] * 2,
                out_specs=(pl.BlockSpec((MOST, part, BLOCK), lambda i, w: (i, 0, 0)),) * 4,
            ),
            compiler_params=params,
            name="core_sum",
        )(where, mine, other)

    def swap(value):
        return lax.ppermute(value, "dp", [(d, d ^ 1) for d in range(groups)])

    mine = [mine_g, mine_u]
    other = [swap(other_g), swap(other_u)]
    sent = [reduced(mine[m], other[m]) for m in range(2)]
    came = [[sent[m][0]] + [around(sent[m][s], s) for s in (1, 2, 3)] for m in range(2)]
    columns = [[x * ring + z for x in range(sides)] for z in range(ring)]
    row_terms = lax.psum_scatter(
        terms, "mp", scatter_dimension=0, axis_index_groups=columns, tiled=True
    )
    returning = pl.pallas_call(
        unsort_kernel,
        out_shape=jax.ShapeDtypeStruct((slots, part, BLOCK), BF16),
        grid_spec=pltpu.PrefetchScalarGridSpec(
            num_scalar_prefetch=2,
            grid=(1,),
            in_specs=[whole(piece.shape)] * 8,
            out_specs=whole((slots, part, BLOCK)),
        ),
        compiler_params=params,
        name="unsort_slots",
    )(table, count, *came[0], *came[1])
    own = pl.pallas_call(
        lambda *refs: own_kernel(panels, *refs),
        out_shape=jax.ShapeDtypeStruct((2, owned, part, BLOCK), BF16),
        grid_spec=pltpu.PrefetchScalarGridSpec(
            num_scalar_prefetch=2,
            grid=(1,),
            in_specs=[whole((slots, part, BLOCK))],
            out_specs=whole((2, owned, part, BLOCK)),
        ),
        compiler_params=params,
        name="own_slots",
    )(where, tile_cols, exchange(returning))
    own = own.reshape(2 * owned, part, BLOCK)
    full = [own] + [around(own, s) for s in (1, 2, 3)]
    full = [v for t in full for v in (t, swap(t))]
    input_grad = lax.psum_scatter(
        row_terms, "mp", scatter_dimension=0, axis_index_groups=rows, tiled=True
    )
    tile_grads, input_grad = pl.pallas_call(
        widen_kernel,
        out_shape=(
            jax.ShapeDtypeStruct((2 * owned, BLOCK, BLOCK), F32),
            jax.ShapeDtypeStruct(tokens.shape, BF16),
        ),
        grid_spec=pltpu.PrefetchScalarGridSpec(
            num_scalar_prefetch=1,
            grid=(1,),
            in_specs=[anywhere] * groups + [whole((my_blocks, tok_rows, BLOCK))],
            out_specs=(anywhere, whole(tokens.shape)),
            scratch_shapes=[
                pltpu.VMEM((groups, 2 * owned, part, BLOCK), BF16),
                pltpu.VMEM((2 * owned, BLOCK, BLOCK), F32),
                pltpu.SemaphoreType.DMA((groups, 2)),
                pltpu.SemaphoreType.DMA((6,)),
            ],
        ),
        compiler_params=alone,
        name="widen",
    )(where, *full, input_grad)
    tile_grads = tile_grads.reshape(tiles.shape)
    return hidden, input_grad, tile_grads


def solution(mesh):
    in_specs = (P("dp", "mp"), P("dp", "mp"), P(None, "mp", None, None), P(), P())
    out_specs = (P("dp", "mp"), P("dp", "mp"), P(None, "mp", None, None))
    return jax.shard_map(
        per_device, mesh=mesh, in_specs=in_specs, out_specs=out_specs, check_vma=False
    )
```

```python
import jax
import jax.numpy as jnp
from jax import lax
from jax.experimental import pallas as pl
from jax.experimental.pallas import tpu as pltpu
from jax.sharding import PartitionSpec as P

BLOCK = 128
MOST = 12
PAIR = 3
GROUP = 4
F32 = jnp.float32
BF16 = jnp.bfloat16


def nt(a, b):
    return lax.dot_general(a, b, (((1,), (1,)), ((), ())), preferred_element_type=F32)


def nn(a, b):
    return lax.dot_general(a, b, (((1,), (0,)), ((), ())), preferred_element_type=F32)


def slot_table(tile_rows, tile_cols, me, members, panels):
    owned = tile_cols.shape[1] // members
    cols = tile_cols.reshape(2, members, owned)
    rows = tile_rows.reshape(2, members, owned)
    local = cols - me * panels
    holder = cols // panels
    pad = jnp.full((2, members, 2), -1, jnp.int32)

    def run(values):
        one = jnp.concatenate([pad[:, :, :1], values[:, :, :-1]], axis=2)
        two = jnp.concatenate([pad, values[:, :, :-2]], axis=2)
        return (values == one).astype(jnp.int32) + (values == two).astype(jnp.int32)

    rank = run(holder)
    within = run(cols)
    value = jnp.arange(members)[None, :, None] * 256 + rank * 64 + rows
    mine = local[None] == jnp.arange(panels)[:, None, None, None]
    count = jnp.sum(mine.astype(jnp.int32), axis=3)
    before = jnp.arange(members)[:, None] > jnp.arange(members)[None, :]
    earlier = jnp.sum(jnp.where(before, count[:, :, None, :], 0), axis=3)
    place_in_panel = jnp.where(mine, earlier[..., None] + within[None], -1)
    hit = place_in_panel[:, :, None] == jnp.arange(MOST)[:, None, None]
    table = jnp.sum(jnp.where(hit, value[None, :, None], 0), axis=(3, 4))
    return jnp.swapaxes(table, 0, 1).reshape(-1), jnp.sum(count, axis=2).T.reshape(-1)


def slot_of(cols_ref, me, owned, panels, m, visit):
    by = 65536 // panels + 1

    def step(k, carry):
        last, rank = carry
        holder = (cols_ref[m, me * owned + k] * by) >> 16
        rank = jnp.where(holder == last, rank + 1, 0)
        visit(k, holder, rank)
        return holder, rank

    lax.fori_loop(0, owned, step, (jnp.int32(-1), jnp.int32(0)), unroll=7)


def send_kernel(panels, place_ref, cols_ref, tiles_ref, tokens_ref, out_ref, blocks_ref):
    for m in range(2):

        def visit(k, holder, rank):
            out_ref[holder * (2 * PAIR) + m * PAIR + rank] = tiles_ref[m, k]

        slot_of(cols_ref, place_ref[0], tiles_ref.shape[1], panels, m, visit)
    for b in range(blocks_ref.shape[0]):
        blocks_ref[b] = tokens_ref[:, b * BLOCK : (b + 1) * BLOCK]


def own_kernel(panels, place_ref, cols_ref, back_ref, out_ref):
    for m in range(2):

        def visit(k, holder, rank):
            out_ref[m, k] = back_ref[holder * (2 * PAIR) + m * PAIR + rank]

        slot_of(cols_ref, place_ref[0], out_ref.shape[1], panels, m, visit)


def sort_kernel(table_ref, in_ref, out_ref):
    half = out_ref.shape[0] // 2
    for m in range(2):

        def step(s, carry):
            v = table_ref[m * half + s]
            out_ref[m * half + s] = in_ref[(v >> 8) * (2 * PAIR) + m * PAIR + ((v >> 6) & 3)]
            return carry

        lax.fori_loop(0, half, step, 0, unroll=6)


def unsort_kernel(table_ref, count_ref, *refs):
    out_ref = refs[-1]
    each = len(refs) // 2
    half = refs[0].shape[0]
    panels = half // MOST
    for m in range(2):
        in_refs = refs[m * each : (m + 1) * each]
        for q in range(panels):

            def step(g, carry):
                for i in range(GROUP):
                    s = q * MOST + g * GROUP + i
                    v = table_ref[m * half + s]
                    total = sum(r[s].astype(F32) for r in in_refs).astype(BF16)
                    out_ref[(v >> 8) * (2 * PAIR) + m * PAIR + ((v >> 6) & 3)] = total
                return carry

            lax.fori_loop(0, count_ref[m * panels + q] // GROUP, step, 0)


def core_kernel(where_ref, mine_ref, other_ref, *out_refs):
    for k, out_ref in enumerate(out_refs):
        y = lax.rem(where_ref[5] + k, 4)
        out_ref[...] = (mine_ref[y].astype(F32) + other_ref[y].astype(F32)).astype(BF16)


def main_kernel(sides, ring, panels, table_ref, count_ref, where_ref, *refs):
    pieces, refs = refs[: ring + 1], refs[ring + 1 :]
    tile_hbm, cot_ref, hidden_ref, *refs = refs
    grads_hbm, refs = (refs[:2], refs[2:4]), refs[4:]
    terms_ref, tok_ref, tok_t, total, tile_ref, grad_ref, pair_ref, *refs = refs
    tok_sems, in_sems, out_sems = refs
    blocks = tok_ref.shape[0]
    each = blocks // sides
    turned = -(-blocks // panels)
    side = where_ref[2]

    core = where_ref[4]

    def loads(p):
        for m in range(2):
            at = pl.ds((m * panels + p) * MOST, MOST)
            yield pltpu.make_async_copy(tile_hbm.at[:, at], tile_ref.at[:, at], in_sems.at[m, p])

    def stores(p):
        for m in range(2):
            at, to = pl.ds((m * panels + p) * MOST, MOST), pl.ds(p * MOST, MOST)
            for k in range(2):
                yield pltpu.make_async_copy(
                    grad_ref.at[k, :, at], grads_hbm[k][m].at[:, to], out_sems.at[k, m, p]
                )

    steps = [j for j in range(ring) if j != ring // 2]
    held = [(j, s, piece.at[s]) for j, piece in zip(steps, pieces) for s in range(sides)]
    held += [
        (ring // 2, k * sides // 2 + s, piece.at[s])
        for k, piece in enumerate(pieces[-2:])
        for s in range(sides // 2)
    ]
    copies = [
        pltpu.make_async_copy(
            piece,
            tok_ref.at[
                pl.ds(
                    lax.rem(side + sides - s, sides) * each
                    + lax.rem(where_ref[3] + ring - j, ring) * (each // ring),
                    each // ring,
                )
            ],
            tok_sems.at[s, j],
        )
        for j, s, piece in held
    ]
    for copy in copies:
        copy.start()
    for p in range(panels):
        for copy in loads(p):
            copy.start()

    def clear(b, carry):
        total[b] = jnp.zeros_like(total[b])
        return carry

    lax.fori_loop(0, blocks, clear, 0)
    for copy in copies:
        copy.wait()

    def stacked(p, m, first):
        w = tile_ref[:, pl.ds((m * panels + p) * MOST + first, GROUP)]
        return jnp.concatenate([w[:, i].reshape(BLOCK, BLOCK) for i in range(GROUP)], axis=0)

    def by_counts(p, work):
        many = [count_ref[m * panels + p] > GROUP for m in range(2)]
        for most in range(4):
            picked = [bool(most & 1), bool(most & 2)]
            same = [many[m] if picked[m] else jnp.logical_not(many[m]) for m in range(2)]

            @pl.when(jnp.logical_and(same[0], same[1]))
            def _():
                counts = [MOST if picked[m] else GROUP for m in range(2)]
                at = [
                    [table_ref[(m * panels + p) * MOST + t] & 63 for t in range(counts[m])]
                    for m in range(2)
                ]
                work(p, counts, at)

    def forward(p, counts, at):
        for i in range(turned):
            b = jnp.minimum(p * turned + i, blocks - 1)
            tok_t[b] = tok_ref[b].T
        pre = []
        for m in range(2):
            acc = None
            for first in range(0, counts[m], GROUP):
                lhs = jnp.concatenate([tok_ref[at[m][first + i]] for i in range(GROUP)], axis=1)
                term = nn(lhs, stacked(p, m, first))
                acc = term if acc is None else acc + term
            pre.append(acc)
        gate, up = pre
        sig = 1.0 / (1.0 + jnp.exp(-gate))
        columns = pl.ds(pl.multiple_of(p * BLOCK, BLOCK), BLOCK)
        hidden_ref[:, columns] = (gate * sig * up).astype(BF16)
        cot = cot_ref[:, columns].astype(F32)
        pair_ref[p * 2] = (cot * up * sig * (1.0 + gate * (1.0 - sig))).astype(BF16)
        pair_ref[p * 2 + 1] = (cot * gate * sig).astype(BF16)

    def backward(p, counts, at):
        for m in range(2):
            grad = pair_ref[p * 2 + m]
            for first in range(0, counts[m], GROUP):
                lhs = jnp.concatenate([tok_t[at[m][first + i]] for i in range(GROUP)], axis=0)
                out = nn(lhs, grad).astype(BF16)
                back = nt(grad, stacked(p, m, first))
                for i in range(GROUP):
                    part = out[i * BLOCK : (i + 1) * BLOCK].reshape(4, 2, BLOCK // 8, BLOCK)
                    slot = (m * panels + p) * MOST + first + i
                    grad_ref[core, :, slot] = part[:, 0]
                    grad_ref[1 - core, :, slot] = part[:, 1]
                    total[at[m][first + i]] += back[:, i * BLOCK : (i + 1) * BLOCK]

    def first_pass(p, carry):
        for copy in loads(p):
            copy.wait()
        by_counts(p, forward)
        return carry

    def second_pass(p, carry):
        by_counts(p, backward)
        for copy in stores(p):
            copy.start()
        return carry

    lax.fori_loop(0, panels, first_pass, 0)
    lax.fori_loop(0, panels, second_pass, 0)

    def step(b, carry):
        terms_ref[b] = total[b].astype(BF16)
        return carry

    lax.fori_loop(0, blocks, step, 0, unroll=2)
    for p in range(panels):
        for copy in stores(p):
            copy.wait()


def widen_kernel(where_ref, *refs):
    pieces, (blocks_ref, out_hbm, flat_ref, out_ref, sems) = refs[:-5], refs[-5:]
    count, part, _ = pieces[0].shape
    stores = sems.shape[0]
    some = count // stores
    core, y = where_ref[4], where_ref[5]

    def store(i):
        at = pl.ds(i * some, some)
        return pltpu.make_async_copy(out_ref.at[at], out_hbm.at[at], sems.at[i])

    for i in range(stores):
        for k, piece in enumerate(pieces):
            chunk = lax.rem(y + 4 - k // 2, 4) * 2 + (1 - core if k % 2 else core)
            rows = pl.ds(pl.multiple_of(chunk * part, part), part)
            out_ref[i * some : (i + 1) * some, rows, :] = piece[i * some : (i + 1) * some].astype(F32)
        store(i).start()
    for b in range(blocks_ref.shape[0]):
        flat_ref[:, b * BLOCK : (b + 1) * BLOCK] = blocks_ref[b]
    for i in range(stores):
        store(i).wait()


def whole(shape):
    return pl.BlockSpec(shape, lambda *_: (0,) * len(shape))


def per_device(tokens, cotangent, tiles, tile_rows, tile_cols):
    groups = lax.axis_size("dp")
    members = lax.axis_size("mp")
    me = lax.axis_index("mp")
    mygroup = lax.axis_index("dp")
    owned = tiles.shape[1]
    tok_rows, my_features = tokens.shape
    my_blocks = my_features // BLOCK
    row_blocks = my_blocks * members
    panels = cotangent.shape[1] // BLOCK
    part = BLOCK // groups
    slots = members * 2 * PAIR
    used = panels * 2 * MOST
    params = pltpu.CompilerParams(vmem_limit_bytes=48 * 1024 * 1024)
    less = pltpu.CompilerParams(vmem_limit_bytes=24 * 1024 * 1024)
    alone = pltpu.CompilerParams(vmem_limit_bytes=60 * 1024 * 1024)
    sides = 4
    ring = members // sides
    each = row_blocks // sides
    where = jnp.stack([me, mygroup, me // ring, me % ring, mygroup % 2, mygroup // 2]).astype(jnp.int32)

    outgoing, my_tok = pl.pallas_call(
        lambda *refs: send_kernel(panels, *refs),
        out_shape=(
            jax.ShapeDtypeStruct((slots, part, BLOCK), BF16),
            jax.ShapeDtypeStruct((my_blocks, tok_rows, BLOCK), BF16),
        ),
        grid_spec=pltpu.PrefetchScalarGridSpec(
            num_scalar_prefetch=2,
            grid=(1,),
            in_specs=[
                pl.BlockSpec((2, owned, part, BLOCK), lambda i, w, c: (0, 0, w[1], 0)),
                whole(tokens.shape),
            ],
            out_specs=(whole((slots, part, BLOCK)), whole((my_blocks, tok_rows, BLOCK))),
        ),
        compiler_params=alone,
        name="send_pack",
    )(where, tile_cols, tiles, tokens)

    def exchange(values):
        shape = (members, -1) + values.shape[1:]
        return lax.all_to_all(values.reshape(shape), "mp", 0, 0).reshape(values.shape)

    rows = [[x * ring + z for z in range(ring)] for x in range(sides)]

    def turn(value, s):
        pairs = [
            (x * ring + z, (x + s) % sides * ring + z) for x in range(sides) for z in range(ring)
        ]
        return lax.ppermute(value, "mp", pairs)

    def along(value, s):
        pairs = [
            (x * ring + z, x * ring + (z + s) % ring) for x in range(sides) for z in range(ring)
        ]
        return lax.ppermute(value, "mp", pairs)

    line_tok = jnp.stack([my_tok] + [turn(my_tok, s) for s in range(1, sides)])
    table, count = slot_table(tile_rows, tile_cols, me, members, panels)
    incoming, line_tok = lax.optimization_barrier((exchange(outgoing), line_tok))
    ordered = pl.pallas_call(
        sort_kernel,
        out_shape=jax.ShapeDtypeStruct((used, part, BLOCK), BF16),
        grid_spec=pltpu.PrefetchScalarGridSpec(
            num_scalar_prefetch=1,
            grid=(1,),
            in_specs=[whole((slots, part, BLOCK))],
            out_specs=whole((used, part, BLOCK)),
        ),
        compiler_params=params,
        name="sort_slots",
    )(table, incoming)
    held = lax.all_gather(ordered, "dp")
    ups, downs = [line_tok], [line_tok]
    for _ in range(ring // 2 - 1):
        ups.append(along(ups[-1], 1))
        downs.append(along(downs[-1], -1))
    far = [along(ups[-1][: sides // 2], 1), along(downs[-1][sides // 2 :], -1)]
    pieces = ups + downs[:0:-1] + far

    anywhere = pl.BlockSpec(memory_space=pl.ANY)
    split = jax.ShapeDtypeStruct((4, used // 2, part, BLOCK), BF16)
    hidden, mine_g, mine_u, other_g, other_u, terms = pl.pallas_call(
        lambda *refs: main_kernel(sides, ring, panels, *refs),
        out_shape=(
            jax.ShapeDtypeStruct(cotangent.shape, BF16),
            *(split,) * 4,
        )
        + (jax.ShapeDtypeStruct((row_blocks, tok_rows, BLOCK), BF16),),
        grid_spec=pltpu.PrefetchScalarGridSpec(
            num_scalar_prefetch=3,
            grid=(1,),
            in_specs=[anywhere] * (len(pieces) + 1) + [whole(cotangent.shape)],
            out_specs=(whole(cotangent.shape), *(anywhere,) * 4)
            + (whole((row_blocks, tok_rows, BLOCK)),),
            scratch_shapes=[
                pltpu.VMEM((row_blocks, tok_rows, BLOCK), BF16),
                pltpu.VMEM((row_blocks, BLOCK, tok_rows), BF16),
                pltpu.VMEM((row_blocks, tok_rows, BLOCK), F32),
                pltpu.VMEM((groups, used, part, BLOCK), BF16),
                pltpu.VMEM((2, 4, used, part, BLOCK), BF16),
                pltpu.VMEM((2 * panels, tok_rows, BLOCK), BF16),
                pltpu.SemaphoreType.DMA((sides, ring)),
                pltpu.SemaphoreType.DMA((2, panels)),
                pltpu.SemaphoreType.DMA((2, 2, panels)),
            ],
        ),
        compiler_params=alone,
        name="gated_pair",
    )(table, count, where, *pieces, held, cotangent)

    def around(value, s):
        pairs = [(y * 2 + c, (y + s) % 4 * 2 + c) for y in range(4) for c in range(2)]
        return lax.ppermute(value, "dp", pairs)

    piece = jax.ShapeDtypeStruct((used // 2, part, BLOCK), BF16)

    def reduced(mine, other):
        block = pl.BlockSpec((4, MOST, part, BLOCK), lambda i, w: (0, i, 0, 0))
        return pl.pallas_call(
            core_kernel,
            out_shape=(piece,) * 4,
            grid_spec=pltpu.PrefetchScalarGridSpec(
                num_scalar_prefetch=1,
                grid=(panels,),
                in_specs=[block] * 2,
                out_specs=(pl.BlockSpec((MOST, part, BLOCK), lambda i, w: (i, 0, 0)),) * 4,
            ),
            compiler_params=params,
            name="core_sum",
        )(where, mine, other)

    def swap(value):
        return lax.ppermute(value, "dp", [(d, d ^ 1) for d in range(groups)])

    mine = [mine_g, mine_u]
    other = [swap(other_g), swap(other_u)]
    sent = [reduced(mine[m], other[m]) for m in range(2)]
    came = [[sent[m][0]] + [around(sent[m][s], s) for s in (2, 1, 3)] for m in range(2)]
    columns = [[x * ring + z for x in range(sides)] for z in range(ring)]
    row_terms = lax.psum_scatter(
        terms, "mp", scatter_dimension=0, axis_index_groups=columns, tiled=True
    )
    returning = pl.pallas_call(
        unsort_kernel,
        out_shape=jax.ShapeDtypeStruct((slots, part, BLOCK), BF16),
        grid_spec=pltpu.PrefetchScalarGridSpec(
            num_scalar_prefetch=2,
            grid=(1,),
            in_specs=[whole(piece.shape)] * 8,
            out_specs=whole((slots, part, BLOCK)),
        ),
        compiler_params=less,
        name="unsort_slots",
    )(table, count, *came[0], *came[1])
    own = pl.pallas_call(
        lambda *refs: own_kernel(panels, *refs),
        out_shape=jax.ShapeDtypeStruct((2, owned, part, BLOCK), BF16),
        grid_spec=pltpu.PrefetchScalarGridSpec(
            num_scalar_prefetch=2,
            grid=(1,),
            in_specs=[whole((slots, part, BLOCK))],
            out_specs=whole((2, owned, part, BLOCK)),
        ),
        compiler_params=params,
        name="own_slots",
    )(where, tile_cols, exchange(returning))
    own = own.reshape(2 * owned, part, BLOCK)
    far, near, back = (around(own, s) for s in (2, 1, 3))
    full = [own, near, far, back]
    full = [v for t in full for v in (t, swap(t))]
    input_grad = lax.psum_scatter(
        row_terms, "mp", scatter_dimension=0, axis_index_groups=rows, tiled=True
    )
    tile_grads, input_grad = pl.pallas_call(
        widen_kernel,
        out_shape=(
            jax.ShapeDtypeStruct((2 * owned, BLOCK, BLOCK), F32),
            jax.ShapeDtypeStruct(tokens.shape, BF16),
        ),
        grid_spec=pltpu.PrefetchScalarGridSpec(
            num_scalar_prefetch=1,
            grid=(1,),
            in_specs=[whole((2 * owned, part, BLOCK))] * groups
            + [whole((my_blocks, tok_rows, BLOCK))],
            out_specs=(anywhere, whole(tokens.shape)),
            scratch_shapes=[
                pltpu.VMEM((2 * owned, BLOCK, BLOCK), F32),
                pltpu.SemaphoreType.DMA((6,)),
            ],
        ),
        compiler_params=less,
        name="widen",
    )(where, *full, input_grad)
    tile_grads = tile_grads.reshape(tiles.shape)
    return hidden, input_grad, tile_grads


def solution(mesh):
    in_specs = (P("dp", "mp"), P("dp", "mp"), P(None, "mp", None, None), P(), P())
    out_specs = (P("dp", "mp"), P("dp", "mp"), P(None, "mp", None, None))
    return jax.shard_map(
        per_device, mesh=mesh, in_specs=in_specs, out_specs=out_specs, check_vma=False
    )
```

```python
import jax
import jax.numpy as jnp
from jax import lax
from jax.experimental import pallas as pl
from jax.experimental.pallas import tpu as pltpu
from jax.sharding import PartitionSpec as P

BLOCK = 128
MOST = 12
PAIR = 3
GROUP = 4
F32 = jnp.float32
BF16 = jnp.bfloat16


def nt(a, b):
    return lax.dot_general(a, b, (((1,), (1,)), ((), ())), preferred_element_type=F32)


def nn(a, b):
    return lax.dot_general(a, b, (((1,), (0,)), ((), ())), preferred_element_type=F32)


def slot_table(tile_rows, tile_cols, me, members, panels):
    owned = tile_cols.shape[1] // members
    cols = tile_cols.reshape(2, members, owned)
    rows = tile_rows.reshape(2, members, owned)
    local = cols - me * panels
    holder = cols // panels
    pad = jnp.full((2, members, 2), -1, jnp.int32)

    def run(values):
        one = jnp.concatenate([pad[:, :, :1], values[:, :, :-1]], axis=2)
        two = jnp.concatenate([pad, values[:, :, :-2]], axis=2)
        return (values == one).astype(jnp.int32) + (values == two).astype(jnp.int32)

    rank = run(holder)
    within = run(cols)
    value = jnp.arange(members)[None, :, None] * 256 + rank * 64 + rows
    mine = local[None] == jnp.arange(panels)[:, None, None, None]
    count = jnp.sum(mine.astype(jnp.int32), axis=3)
    before = jnp.arange(members)[:, None] > jnp.arange(members)[None, :]
    earlier = jnp.sum(jnp.where(before, count[:, :, None, :], 0), axis=3)
    place_in_panel = jnp.where(mine, earlier[..., None] + within[None], -1)
    hit = place_in_panel[:, :, None] == jnp.arange(MOST)[:, None, None]
    table = jnp.sum(jnp.where(hit, value[None, :, None], 0), axis=(3, 4))
    return jnp.swapaxes(table, 0, 1).reshape(-1), jnp.sum(count, axis=2).T.reshape(-1)


def slot_of(cols_ref, me, owned, panels, m, visit):
    by = 65536 // panels + 1

    def step(k, carry):
        last, rank = carry
        holder = (cols_ref[m, me * owned + k] * by) >> 16
        rank = jnp.where(holder == last, rank + 1, 0)
        visit(k, holder, rank)
        return holder, rank

    lax.fori_loop(0, owned, step, (jnp.int32(-1), jnp.int32(0)), unroll=7)


def send_kernel(panels, cols_ref, tiles_ref, tokens_ref, out_ref, blocks_ref):
    for m in range(2):

        def visit(k, holder, rank):
            out_ref[holder * (2 * PAIR) + m * PAIR + rank] = tiles_ref[m, k]

        slot_of(cols_ref, lax.axis_index("mp"), tiles_ref.shape[1], panels, m, visit)
    for b in range(blocks_ref.shape[0]):
        blocks_ref[b] = tokens_ref[:, b * BLOCK : (b + 1) * BLOCK]


def own_kernel(panels, place_ref, cols_ref, back_ref, out_ref):
    for m in range(2):

        def visit(k, holder, rank):
            out_ref[m, k] = back_ref[holder * (2 * PAIR) + m * PAIR + rank]

        slot_of(cols_ref, place_ref[0], out_ref.shape[1], panels, m, visit)


def sort_kernel(table_ref, in_ref, out_ref):
    half = out_ref.shape[0] // 2
    for m in range(2):

        def step(s, carry):
            v = table_ref[m * half + s]
            out_ref[m * half + s] = in_ref[(v >> 8) * (2 * PAIR) + m * PAIR + ((v >> 6) & 3)]
            return carry

        lax.fori_loop(0, half, step, 0, unroll=6)


def unsort_kernel(table_ref, count_ref, *refs):
    out_ref = refs[-1]
    each = len(refs) // 2
    half = refs[0].shape[0]
    panels = half // MOST
    for m in range(2):
        in_refs = refs[m * each : (m + 1) * each]
        for q in range(panels):

            def step(g, carry):
                for i in range(GROUP):
                    s = q * MOST + g * GROUP + i
                    v = table_ref[m * half + s]
                    total = sum(r[s].astype(F32) for r in in_refs).astype(BF16)
                    out_ref[(v >> 8) * (2 * PAIR) + m * PAIR + ((v >> 6) & 3)] = total
                return carry

            lax.fori_loop(0, count_ref[m * panels + q] // GROUP, step, 0)


def core_kernel(where_ref, mine_ref, other_ref, *out_refs):
    for k, out_ref in enumerate(out_refs):
        y = lax.rem(where_ref[5] + k, 4)
        out_ref[...] = (mine_ref[y].astype(F32) + other_ref[y].astype(F32)).astype(BF16)


def main_kernel(sides, ring, panels, table_ref, count_ref, where_ref, *refs):
    pieces, refs = refs[: ring + 1], refs[ring + 1 :]
    tile_hbm, cot_ref, hidden_ref, *refs = refs
    grads_hbm, refs = (refs[:2], refs[2:4]), refs[4:]
    terms_ref, tok_ref, tok_t, total, tile_ref, grad_ref, pair_ref, *refs = refs
    tok_sems, in_sems, out_sems = refs
    blocks = tok_ref.shape[0]
    each = blocks // sides
    turned = -(-blocks // panels)
    side = where_ref[2]

    core = where_ref[4]

    def loads(p):
        for m in range(2):
            at = pl.ds((m * panels + p) * MOST, MOST)
            yield pltpu.make_async_copy(tile_hbm.at[:, at], tile_ref.at[:, at], in_sems.at[m, p])

    def stores(p):
        for m in range(2):
            at, to = pl.ds((m * panels + p) * MOST, MOST), pl.ds(p * MOST, MOST)
            for k in range(2):
                yield pltpu.make_async_copy(
                    grad_ref.at[k, :, at], grads_hbm[k][m].at[:, to], out_sems.at[k, m, p]
                )

    steps = [j for j in range(ring) if j != ring // 2]
    held = [(j, s, piece.at[s]) for j, piece in zip(steps, pieces) for s in range(sides)]
    held += [
        (ring // 2, k * sides // 2 + s, piece.at[s])
        for k, piece in enumerate(pieces[-2:])
        for s in range(sides // 2)
    ]
    copies = [
        pltpu.make_async_copy(
            piece,
            tok_ref.at[
                pl.ds(
                    lax.rem(side + sides - s, sides) * each
                    + lax.rem(where_ref[3] + ring - j, ring) * (each // ring),
                    each // ring,
                )
            ],
            tok_sems.at[s, j],
        )
        for j, s, piece in held
    ]
    for copy in copies:
        copy.start()
    for p in range(panels):
        for copy in loads(p):
            copy.start()

    def clear(b, carry):
        total[b] = jnp.zeros_like(total[b])
        return carry

    lax.fori_loop(0, blocks, clear, 0)
    for copy in copies:
        copy.wait()

    def stacked(p, m, first):
        w = tile_ref[:, pl.ds((m * panels + p) * MOST + first, GROUP)]
        return jnp.concatenate([w[:, i].reshape(BLOCK, BLOCK) for i in range(GROUP)], axis=0)

    def by_counts(p, work):
        many = [count_ref[m * panels + p] > GROUP for m in range(2)]
        for most in range(4):
            picked = [bool(most & 1), bool(most & 2)]
            same = [many[m] if picked[m] else jnp.logical_not(many[m]) for m in range(2)]

            @pl.when(jnp.logical_and(same[0], same[1]))
            def _():
                counts = [MOST if picked[m] else GROUP for m in range(2)]
                at = [
                    [table_ref[(m * panels + p) * MOST + t] & 63 for t in range(counts[m])]
                    for m in range(2)
                ]
                work(p, counts, at)

    def forward(p, counts, at):
        for i in range(turned):
            b = jnp.minimum(p * turned + i, blocks - 1)
            tok_t[b] = tok_ref[b].T
        pre = []
        for m in range(2):
            acc = None
            for first in range(0, counts[m], GROUP):
                lhs = jnp.concatenate([tok_ref[at[m][first + i]] for i in range(GROUP)], axis=1)
                term = nn(lhs, stacked(p, m, first))
                acc = term if acc is None else acc + term
            pre.append(acc)
        gate, up = pre
        sig = 1.0 / (1.0 + jnp.exp(-gate))
        columns = pl.ds(pl.multiple_of(p * BLOCK, BLOCK), BLOCK)
        hidden_ref[:, columns] = (gate * sig * up).astype(BF16)
        cot = cot_ref[:, columns].astype(F32)
        pair_ref[p * 2] = (cot * up * sig * (1.0 + gate * (1.0 - sig))).astype(BF16)
        pair_ref[p * 2 + 1] = (cot * gate * sig).astype(BF16)

    def backward(p, counts, at):
        for m in range(2):
            grad = pair_ref[p * 2 + m]
            for first in range(0, counts[m], GROUP):
                lhs = jnp.concatenate([tok_t[at[m][first + i]] for i in range(GROUP)], axis=0)
                out = nn(lhs, grad).astype(BF16)
                back = nt(grad, stacked(p, m, first))
                for i in range(GROUP):
                    part = out[i * BLOCK : (i + 1) * BLOCK].reshape(4, 2, BLOCK // 8, BLOCK)
                    slot = (m * panels + p) * MOST + first + i
                    grad_ref[core, :, slot] = part[:, 0]
                    grad_ref[1 - core, :, slot] = part[:, 1]
                    total[at[m][first + i]] += back[:, i * BLOCK : (i + 1) * BLOCK]

    def first_pass(p, carry):
        for copy in loads(p):
            copy.wait()
        by_counts(p, forward)
        return carry

    def second_pass(p, carry):
        by_counts(p, backward)
        for copy in stores(p):
            copy.start()
        return carry

    lax.fori_loop(0, panels, first_pass, 0)
    lax.fori_loop(0, panels, second_pass, 0)

    def step(b, carry):
        terms_ref[b] = total[b].astype(BF16)
        return carry

    lax.fori_loop(0, blocks, step, 0, unroll=2)
    for p in range(panels):
        for copy in stores(p):
            copy.wait()


def widen_kernel(where_ref, *refs):
    pieces, (blocks_hbm, out_hbm, flat_hbm, out_ref, sems, flat_sems) = refs[:-6], refs[-6:]
    count, part, _ = pieces[0].shape
    stores = sems.shape[0]
    some = count // stores
    core, y = where_ref[4], where_ref[5]

    def store(i):
        at = pl.ds(i * some, some)
        return pltpu.make_async_copy(out_ref.at[at], out_hbm.at[at], sems.at[i])

    flat = [
        pltpu.make_async_copy(
            blocks_hbm.at[b], flat_hbm.at[:, pl.ds(b * BLOCK, BLOCK)], flat_sems.at[b]
        )
        for b in range(flat_sems.shape[0])
    ]
    for copy in flat:
        copy.start()
    for i in range(stores):
        for k, piece in enumerate(pieces):
            chunk = lax.rem(y + 4 - k // 2, 4) * 2 + (1 - core if k % 2 else core)
            rows = pl.ds(pl.multiple_of(chunk * part, part), part)
            out_ref[i * some : (i + 1) * some, rows, :] = piece[i * some : (i + 1) * some].astype(F32)
        store(i).start()
    for i in range(stores):
        store(i).wait()
    for copy in flat:
        copy.wait()


def whole(shape):
    return pl.BlockSpec(shape, lambda *_: (0,) * len(shape))


def per_device(tokens, cotangent, tiles, tile_rows, tile_cols):
    groups = lax.axis_size("dp")
    members = lax.axis_size("mp")
    me = lax.axis_index("mp")
    mygroup = lax.axis_index("dp")
    owned = tiles.shape[1]
    tok_rows, my_features = tokens.shape
    my_blocks = my_features // BLOCK
    row_blocks = my_blocks * members
    panels = cotangent.shape[1] // BLOCK
    part = BLOCK // groups
    slots = members * 2 * PAIR
    used = panels * 2 * MOST
    params = pltpu.CompilerParams(vmem_limit_bytes=48 * 1024 * 1024)
    less = pltpu.CompilerParams(vmem_limit_bytes=24 * 1024 * 1024)
    alone = pltpu.CompilerParams(vmem_limit_bytes=60 * 1024 * 1024)
    sides = 4
    ring = members // sides
    each = row_blocks // sides
    where = jnp.stack([me, mygroup, me // ring, me % ring, mygroup % 2, mygroup // 2]).astype(jnp.int32)

    outgoing, my_tok = pl.pallas_call(
        lambda *refs: send_kernel(panels, *refs),
        out_shape=(
            jax.ShapeDtypeStruct((slots, part, BLOCK), BF16),
            jax.ShapeDtypeStruct((my_blocks, tok_rows, BLOCK), BF16),
        ),
        grid_spec=pltpu.PrefetchScalarGridSpec(
            num_scalar_prefetch=1,
            grid=(1,),
            in_specs=[
                pl.BlockSpec((2, owned, part, BLOCK), lambda i, c: (0, 0, lax.axis_index("dp"), 0)),
                whole(tokens.shape),
            ],
            out_specs=(whole((slots, part, BLOCK)), whole((my_blocks, tok_rows, BLOCK))),
        ),
        compiler_params=alone,
        name="send_pack",
    )(tile_cols, tiles, tokens)

    def exchange(values):
        shape = (members, -1) + values.shape[1:]
        return lax.all_to_all(values.reshape(shape), "mp", 0, 0).reshape(values.shape)

    rows = [[x * ring + z for z in range(ring)] for x in range(sides)]

    def turn(value, s):
        pairs = [
            (x * ring + z, (x + s) % sides * ring + z) for x in range(sides) for z in range(ring)
        ]
        return lax.ppermute(value, "mp", pairs)

    def along(value, s):
        pairs = [
            (x * ring + z, x * ring + (z + s) % ring) for x in range(sides) for z in range(ring)
        ]
        return lax.ppermute(value, "mp", pairs)

    line_tok = jnp.stack([my_tok] + [turn(my_tok, s) for s in range(1, sides)])
    table, count = slot_table(tile_rows, tile_cols, me, members, panels)
    incoming, line_tok = lax.optimization_barrier((exchange(outgoing), line_tok))
    ordered = pl.pallas_call(
        sort_kernel,
        out_shape=jax.ShapeDtypeStruct((used, part, BLOCK), BF16),
        grid_spec=pltpu.PrefetchScalarGridSpec(
            num_scalar_prefetch=1,
            grid=(1,),
            in_specs=[whole((slots, part, BLOCK))],
            out_specs=whole((used, part, BLOCK)),
        ),
        compiler_params=params,
        name="sort_slots",
    )(table, incoming)
    held = lax.all_gather(ordered, "dp")
    ups, downs = [line_tok], [line_tok]
    for _ in range(ring // 2 - 1):
        ups.append(along(ups[-1], 1))
        downs.append(along(downs[-1], -1))
    far = [along(ups[-1][: sides // 2], 1), along(downs[-1][sides // 2 :], -1)]
    pieces = ups + downs[:0:-1] + far

    anywhere = pl.BlockSpec(memory_space=pl.ANY)
    split = jax.ShapeDtypeStruct((4, used // 2, part, BLOCK), BF16)
    hidden, mine_g, mine_u, other_g, other_u, terms = pl.pallas_call(
        lambda *refs: main_kernel(sides, ring, panels, *refs),
        out_shape=(
            jax.ShapeDtypeStruct(cotangent.shape, BF16),
            *(split,) * 4,
        )
        + (jax.ShapeDtypeStruct((row_blocks, tok_rows, BLOCK), BF16),),
        grid_spec=pltpu.PrefetchScalarGridSpec(
            num_scalar_prefetch=3,
            grid=(1,),
            in_specs=[anywhere] * (len(pieces) + 1) + [whole(cotangent.shape)],
            out_specs=(whole(cotangent.shape), *(anywhere,) * 4)
            + (whole((row_blocks, tok_rows, BLOCK)),),
            scratch_shapes=[
                pltpu.VMEM((row_blocks, tok_rows, BLOCK), BF16),
                pltpu.VMEM((row_blocks, BLOCK, tok_rows), BF16),
                pltpu.VMEM((row_blocks, tok_rows, BLOCK), F32),
                pltpu.VMEM((groups, used, part, BLOCK), BF16),
                pltpu.VMEM((2, 4, used, part, BLOCK), BF16),
                pltpu.VMEM((2 * panels, tok_rows, BLOCK), BF16),
                pltpu.SemaphoreType.DMA((sides, ring)),
                pltpu.SemaphoreType.DMA((2, panels)),
                pltpu.SemaphoreType.DMA((2, 2, panels)),
            ],
        ),
        compiler_params=alone,
        name="gated_pair",
    )(table, count, where, *pieces, held, cotangent)

    def around(value, s):
        pairs = [(y * 2 + c, (y + s) % 4 * 2 + c) for y in range(4) for c in range(2)]
        return lax.ppermute(value, "dp", pairs)

    piece = jax.ShapeDtypeStruct((used // 2, part, BLOCK), BF16)

    def reduced(mine, other):
        block = pl.BlockSpec((4, MOST, part, BLOCK), lambda i, w: (0, i, 0, 0))
        return pl.pallas_call(
            core_kernel,
            out_shape=(piece,) * 4,
            grid_spec=pltpu.PrefetchScalarGridSpec(
                num_scalar_prefetch=1,
                grid=(panels,),
                in_specs=[block] * 2,
                out_specs=(pl.BlockSpec((MOST, part, BLOCK), lambda i, w: (i, 0, 0)),) * 4,
            ),
            compiler_params=params,
            name="core_sum",
        )(where, mine, other)

    def swap(value):
        return lax.ppermute(value, "dp", [(d, d ^ 1) for d in range(groups)])

    mine = [mine_g, mine_u]
    other = [swap(other_g), swap(other_u)]
    sent = [reduced(mine[m], other[m]) for m in range(2)]
    came = [[sent[m][0]] + [around(sent[m][s], s) for s in (2, 1, 3)] for m in range(2)]
    columns = [[x * ring + z for x in range(sides)] for z in range(ring)]
    row_terms = lax.psum_scatter(
        terms, "mp", scatter_dimension=0, axis_index_groups=columns, tiled=True
    )
    returning = pl.pallas_call(
        unsort_kernel,
        out_shape=jax.ShapeDtypeStruct((slots, part, BLOCK), BF16),
        grid_spec=pltpu.PrefetchScalarGridSpec(
            num_scalar_prefetch=2,
            grid=(1,),
            in_specs=[whole(piece.shape)] * 8,
            out_specs=whole((slots, part, BLOCK)),
        ),
        compiler_params=less,
        name="unsort_slots",
    )(table, count, *came[0], *came[1])
    own = pl.pallas_call(
        lambda *refs: own_kernel(panels, *refs),
        out_shape=jax.ShapeDtypeStruct((2, owned, part, BLOCK), BF16),
        grid_spec=pltpu.PrefetchScalarGridSpec(
            num_scalar_prefetch=2,
            grid=(1,),
            in_specs=[whole((slots, part, BLOCK))],
            out_specs=whole((2, owned, part, BLOCK)),
        ),
        compiler_params=params,
        name="own_slots",
    )(where, tile_cols, exchange(returning))
    own = own.reshape(2 * owned, part, BLOCK)
    far, near, back = (around(own, s) for s in (2, 1, 3))
    full = [own, near, far, back]
    full = [v for t in full for v in (t, swap(t))]
    input_grad = lax.psum_scatter(
        row_terms, "mp", scatter_dimension=0, axis_index_groups=rows, tiled=True
    )
    tile_grads, input_grad = pl.pallas_call(
        widen_kernel,
        out_shape=(
            jax.ShapeDtypeStruct((2 * owned, BLOCK, BLOCK), F32),
            jax.ShapeDtypeStruct(tokens.shape, BF16),
        ),
        grid_spec=pltpu.PrefetchScalarGridSpec(
            num_scalar_prefetch=1,
            grid=(1,),
            in_specs=[whole((2 * owned, part, BLOCK))] * groups
            + [anywhere],
            out_specs=(anywhere, anywhere),
            scratch_shapes=[
                pltpu.VMEM((2 * owned, BLOCK, BLOCK), F32),
                pltpu.SemaphoreType.DMA((6,)),
                pltpu.SemaphoreType.DMA((my_blocks,)),
            ],
        ),
        compiler_params=less,
        name="widen",
    )(where, *full, input_grad)
    tile_grads = tile_grads.reshape(tiles.shape)
    return hidden, input_grad, tile_grads


def solution(mesh):
    in_specs = (P("dp", "mp"), P("dp", "mp"), P(None, "mp", None, None), P(), P())
    out_specs = (P("dp", "mp"), P("dp", "mp"), P(None, "mp", None, None))
    return jax.shard_map(
        per_device, mesh=mesh, in_specs=in_specs, out_specs=out_specs, check_vma=False
    )
```

```python
import jax
import jax.numpy as jnp
from jax import lax
from jax.experimental import pallas as pl
from jax.experimental.pallas import tpu as pltpu
from jax.sharding import PartitionSpec as P

BLOCK = 128
MOST = 12
PAIR = 3
GROUP = 4
F32 = jnp.float32
BF16 = jnp.bfloat16


def nt(a, b):
    return lax.dot_general(a, b, (((1,), (1,)), ((), ())), preferred_element_type=F32)


def nn(a, b):
    return lax.dot_general(a, b, (((1,), (0,)), ((), ())), preferred_element_type=F32)


def slot_table(tile_rows, tile_cols, me, members, panels):
    owned = tile_cols.shape[1] // members
    cols = tile_cols.reshape(2, members, owned)
    rows = tile_rows.reshape(2, members, owned)
    local = cols - me * panels
    holder = cols // panels
    pad = jnp.full((2, members, 2), -1, jnp.int32)

    def run(values):
        one = jnp.concatenate([pad[:, :, :1], values[:, :, :-1]], axis=2)
        two = jnp.concatenate([pad, values[:, :, :-2]], axis=2)
        return (values == one).astype(jnp.int32) + (values == two).astype(jnp.int32)

    rank = run(holder)
    within = run(cols)
    value = jnp.arange(members)[None, :, None] * 256 + rank * 64 + rows
    mine = local[None] == jnp.arange(panels)[:, None, None, None]
    count = jnp.sum(mine.astype(jnp.int32), axis=3)
    before = jnp.arange(members)[:, None] > jnp.arange(members)[None, :]
    earlier = jnp.sum(jnp.where(before, count[:, :, None, :], 0), axis=3)
    place_in_panel = jnp.where(mine, earlier[..., None] + within[None], -1)
    hit = place_in_panel[:, :, None] == jnp.arange(MOST)[:, None, None]
    table = jnp.sum(jnp.where(hit, value[None, :, None], 0), axis=(3, 4))
    return jnp.swapaxes(table, 0, 1).reshape(-1), jnp.sum(count, axis=2).T.reshape(-1)


def slot_of(cols_ref, me, owned, panels, m, visit):
    by = 65536 // panels + 1

    def step(k, carry):
        last, rank = carry
        holder = (cols_ref[m, me * owned + k] * by) >> 16
        rank = jnp.where(holder == last, rank + 1, 0)
        visit(k, holder, rank)
        return holder, rank

    lax.fori_loop(0, owned, step, (jnp.int32(-1), jnp.int32(0)), unroll=7)


def send_kernel(panels, cols_ref, tiles_ref, tokens_ref, out_ref, blocks_ref):
    for m in range(2):

        def visit(k, holder, rank):
            out_ref[holder * (2 * PAIR) + m * PAIR + rank] = tiles_ref[m, k]

        slot_of(cols_ref, lax.axis_index("mp"), tiles_ref.shape[1], panels, m, visit)
    for b in range(blocks_ref.shape[0]):
        blocks_ref[b] = tokens_ref[:, b * BLOCK : (b + 1) * BLOCK]


def own_kernel(panels, place_ref, cols_ref, back_ref, out_ref):
    for m in range(2):

        def visit(k, holder, rank):
            out_ref[m, k] = back_ref[holder * (2 * PAIR) + m * PAIR + rank]

        slot_of(cols_ref, place_ref[0], out_ref.shape[1], panels, m, visit)


def sort_kernel(table_ref, in_ref, out_ref):
    half = out_ref.shape[0] // 2
    for m in range(2):

        def step(s, carry):
            v = table_ref[m * half + s]
            out_ref[m * half + s] = in_ref[(v >> 8) * (2 * PAIR) + m * PAIR + ((v >> 6) & 3)]
            return carry

        lax.fori_loop(0, half, step, 0, unroll=6)


def unsort_kernel(table_ref, count_ref, *refs):
    out_ref = refs[-1]
    each = len(refs) // 2
    half = refs[0].shape[0]
    panels = half // MOST
    for m in range(2):
        in_refs = refs[m * each : (m + 1) * each]
        for q in range(panels):

            def step(g, carry):
                for i in range(GROUP):
                    s = q * MOST + g * GROUP + i
                    v = table_ref[m * half + s]
                    total = sum(r[s].astype(F32) for r in in_refs).astype(BF16)
                    out_ref[(v >> 8) * (2 * PAIR) + m * PAIR + ((v >> 6) & 3)] = total
                return carry

            lax.fori_loop(0, count_ref[m * panels + q] // GROUP, step, 0)


def core_kernel(where_ref, mine_ref, other_ref, *out_refs):
    for k, out_ref in enumerate(out_refs):
        y = lax.rem(where_ref[5] + k, 4)
        out_ref[...] = (mine_ref[y].astype(F32) + other_ref[y].astype(F32)).astype(BF16)


def relay_kernel(near_ref, back_ref, first_ref, last_ref, near_out, back_out):
    half = first_ref.shape[0]
    near_out[:half] = (near_ref[:half].astype(F32) + first_ref[...].astype(F32)).astype(BF16)
    near_out[half:] = near_ref[half:]
    back_out[:half] = back_ref[:half]
    back_out[half:] = (back_ref[half:].astype(F32) + last_ref[...].astype(F32)).astype(BF16)


def main_kernel(sides, ring, panels, table_ref, count_ref, where_ref, *refs):
    pieces, refs = refs[: ring + 1], refs[ring + 1 :]
    tile_hbm, cot_ref, hidden_ref, *refs = refs
    grads_hbm, refs = (refs[:2], refs[2:4]), refs[4:]
    terms_ref, tok_ref, tok_t, total, tile_ref, grad_ref, pair_ref, *refs = refs
    tok_sems, in_sems, out_sems = refs
    blocks = tok_ref.shape[0]
    each = blocks // sides
    turned = -(-blocks // panels)
    side = where_ref[2]

    core = where_ref[4]

    def loads(p):
        for m in range(2):
            at = pl.ds((m * panels + p) * MOST, MOST)
            yield pltpu.make_async_copy(tile_hbm.at[:, at], tile_ref.at[:, at], in_sems.at[m, p])

    def stores(p):
        for m in range(2):
            at, to = pl.ds((m * panels + p) * MOST, MOST), pl.ds(p * MOST, MOST)
            for k in range(2):
                yield pltpu.make_async_copy(
                    grad_ref.at[k, :, at], grads_hbm[k][m].at[:, to], out_sems.at[k, m, p]
                )

    steps = [j for j in range(ring) if j != ring // 2]
    held = [(j, s, piece.at[s]) for j, piece in zip(steps, pieces) for s in range(sides)]
    held += [
        (ring // 2, k * sides // 2 + s, piece.at[s])
        for k, piece in enumerate(pieces[-2:])
        for s in range(sides // 2)
    ]
    copies = [
        pltpu.make_async_copy(
            piece,
            tok_ref.at[
                pl.ds(
                    lax.rem(side + sides - s, sides) * each
                    + lax.rem(where_ref[3] + ring - j, ring) * (each // ring),
                    each // ring,
                )
            ],
            tok_sems.at[s, j],
        )
        for j, s, piece in held
    ]
    for copy in copies:
        copy.start()
    for p in range(panels):
        for copy in loads(p):
            copy.start()

    def clear(b, carry):
        total[b] = jnp.zeros_like(total[b])
        return carry

    lax.fori_loop(0, blocks, clear, 0)
    for copy in copies:
        copy.wait()

    def stacked(p, m, first):
        w = tile_ref[:, pl.ds((m * panels + p) * MOST + first, GROUP)]
        return jnp.concatenate([w[:, i].reshape(BLOCK, BLOCK) for i in range(GROUP)], axis=0)

    def by_counts(p, work):
        many = [count_ref[m * panels + p] > GROUP for m in range(2)]
        for most in range(4):
            picked = [bool(most & 1), bool(most & 2)]
            same = [many[m] if picked[m] else jnp.logical_not(many[m]) for m in range(2)]

            @pl.when(jnp.logical_and(same[0], same[1]))
            def _():
                counts = [MOST if picked[m] else GROUP for m in range(2)]
                at = [
                    [table_ref[(m * panels + p) * MOST + t] & 63 for t in range(counts[m])]
                    for m in range(2)
                ]
                work(p, counts, at)

    def forward(p, counts, at):
        for i in range(turned):
            b = jnp.minimum(p * turned + i, blocks - 1)
            tok_t[b] = tok_ref[b].T
        pre = []
        for m in range(2):
            acc = None
            for first in range(0, counts[m], GROUP):
                lhs = jnp.concatenate([tok_ref[at[m][first + i]] for i in range(GROUP)], axis=1)
                term = nn(lhs, stacked(p, m, first))
                acc = term if acc is None else acc + term
            pre.append(acc)
        gate, up = pre
        sig = 1.0 / (1.0 + jnp.exp(-gate))
        columns = pl.ds(pl.multiple_of(p * BLOCK, BLOCK), BLOCK)
        hidden_ref[:, columns] = (gate * sig * up).astype(BF16)
        cot = cot_ref[:, columns].astype(F32)
        pair_ref[p * 2] = (cot * up * sig * (1.0 + gate * (1.0 - sig))).astype(BF16)
        pair_ref[p * 2 + 1] = (cot * gate * sig).astype(BF16)

    def backward(p, counts, at):
        for m in range(2):
            grad = pair_ref[p * 2 + m]
            for first in range(0, counts[m], GROUP):
                lhs = jnp.concatenate([tok_t[at[m][first + i]] for i in range(GROUP)], axis=0)
                out = nn(lhs, grad).astype(BF16)
                back = nt(grad, stacked(p, m, first))
                for i in range(GROUP):
                    part = out[i * BLOCK : (i + 1) * BLOCK].reshape(4, 2, BLOCK // 8, BLOCK)
                    slot = (m * panels + p) * MOST + first + i
                    grad_ref[core, :, slot] = part[:, 0]
                    grad_ref[1 - core, :, slot] = part[:, 1]
                    total[at[m][first + i]] += back[:, i * BLOCK : (i + 1) * BLOCK]

    def first_pass(p, carry):
        for copy in loads(p):
            copy.wait()
        by_counts(p, forward)
        return carry

    def second_pass(p, carry):
        by_counts(p, backward)
        for copy in stores(p):
            copy.start()
        return carry

    lax.fori_loop(0, panels, first_pass, 0)
    lax.fori_loop(0, panels, second_pass, 0)

    def step(b, carry):
        terms_ref[b] = total[b].astype(BF16)
        return carry

    lax.fori_loop(0, blocks, step, 0, unroll=2)
    for p in range(panels):
        for copy in stores(p):
            copy.wait()


def widen_kernel(where_ref, *refs):
    pieces, (blocks_hbm, out_hbm, flat_hbm, out_ref, sems, flat_sems) = refs[:-6], refs[-6:]
    count, part, _ = pieces[0].shape
    stores = sems.shape[0]
    some = count // stores
    core, y = where_ref[4], where_ref[5]

    def store(i):
        at = pl.ds(i * some, some)
        return pltpu.make_async_copy(out_ref.at[at], out_hbm.at[at], sems.at[i])

    flat = [
        pltpu.make_async_copy(
            blocks_hbm.at[b], flat_hbm.at[:, pl.ds(b * BLOCK, BLOCK)], flat_sems.at[b]
        )
        for b in range(flat_sems.shape[0])
    ]
    for copy in flat:
        copy.start()
    for i in range(stores):
        for k, piece in enumerate(pieces):
            chunk = lax.rem(y + 4 - k // 2, 4) * 2 + (1 - core if k % 2 else core)
            rows = pl.ds(pl.multiple_of(chunk * part, part), part)
            out_ref[i * some : (i + 1) * some, rows, :] = piece[i * some : (i + 1) * some].astype(F32)
        store(i).start()
    for i in range(stores):
        store(i).wait()
    for copy in flat:
        copy.wait()


def whole(shape):
    return pl.BlockSpec(shape, lambda *_: (0,) * len(shape))


def per_device(tokens, cotangent, tiles, tile_rows, tile_cols):
    groups = lax.axis_size("dp")
    members = lax.axis_size("mp")
    me = lax.axis_index("mp")
    mygroup = lax.axis_index("dp")
    owned = tiles.shape[1]
    tok_rows, my_features = tokens.shape
    my_blocks = my_features // BLOCK
    row_blocks = my_blocks * members
    panels = cotangent.shape[1] // BLOCK
    part = BLOCK // groups
    slots = members * 2 * PAIR
    used = panels * 2 * MOST
    params = pltpu.CompilerParams(vmem_limit_bytes=48 * 1024 * 1024)
    less = pltpu.CompilerParams(vmem_limit_bytes=24 * 1024 * 1024)
    alone = pltpu.CompilerParams(vmem_limit_bytes=60 * 1024 * 1024)
    sides = 4
    ring = members // sides
    each = row_blocks // sides
    where = jnp.stack([me, mygroup, me // ring, me % ring, mygroup % 2, mygroup // 2]).astype(jnp.int32)

    outgoing, my_tok = pl.pallas_call(
        lambda *refs: send_kernel(panels, *refs),
        out_shape=(
            jax.ShapeDtypeStruct((slots, part, BLOCK), BF16),
            jax.ShapeDtypeStruct((my_blocks, tok_rows, BLOCK), BF16),
        ),
        grid_spec=pltpu.PrefetchScalarGridSpec(
            num_scalar_prefetch=1,
            grid=(1,),
            in_specs=[
                pl.BlockSpec((2, owned, part, BLOCK), lambda i, c: (0, 0, lax.axis_index("dp"), 0)),
                whole(tokens.shape),
            ],
            out_specs=(whole((slots, part, BLOCK)), whole((my_blocks, tok_rows, BLOCK))),
        ),
        compiler_params=alone,
        name="send_pack",
    )(tile_cols, tiles, tokens)

    def exchange(values):
        shape = (members, -1) + values.shape[1:]
        return lax.all_to_all(values.reshape(shape), "mp", 0, 0).reshape(values.shape)

    rows = [[x * ring + z for z in range(ring)] for x in range(sides)]

    def turn(value, s):
        pairs = [
            (x * ring + z, (x + s) % sides * ring + z) for x in range(sides) for z in range(ring)
        ]
        return lax.ppermute(value, "mp", pairs)

    def along(value, s):
        pairs = [
            (x * ring + z, x * ring + (z + s) % ring) for x in range(sides) for z in range(ring)
        ]
        return lax.ppermute(value, "mp", pairs)

    line_tok = jnp.stack([my_tok] + [turn(my_tok, s) for s in range(1, sides)])
    table, count = slot_table(tile_rows, tile_cols, me, members, panels)
    incoming, line_tok = lax.optimization_barrier((exchange(outgoing), line_tok))
    ordered = pl.pallas_call(
        sort_kernel,
        out_shape=jax.ShapeDtypeStruct((used, part, BLOCK), BF16),
        grid_spec=pltpu.PrefetchScalarGridSpec(
            num_scalar_prefetch=1,
            grid=(1,),
            in_specs=[whole((slots, part, BLOCK))],
            out_specs=whole((used, part, BLOCK)),
        ),
        compiler_params=params,
        name="sort_slots",
    )(table, incoming)
    held = lax.all_gather(ordered, "dp")
    ups, downs = [line_tok], [line_tok]
    for _ in range(ring // 2 - 1):
        ups.append(along(ups[-1], 1))
        downs.append(along(downs[-1], -1))
    far = [along(ups[-1][: sides // 2], 1), along(downs[-1][sides // 2 :], -1)]
    pieces = ups + downs[:0:-1] + far

    anywhere = pl.BlockSpec(memory_space=pl.ANY)
    split = jax.ShapeDtypeStruct((4, used // 2, part, BLOCK), BF16)
    hidden, mine_g, mine_u, other_g, other_u, terms = pl.pallas_call(
        lambda *refs: main_kernel(sides, ring, panels, *refs),
        out_shape=(
            jax.ShapeDtypeStruct(cotangent.shape, BF16),
            *(split,) * 4,
        )
        + (jax.ShapeDtypeStruct((row_blocks, tok_rows, BLOCK), BF16),),
        grid_spec=pltpu.PrefetchScalarGridSpec(
            num_scalar_prefetch=3,
            grid=(1,),
            in_specs=[anywhere] * (len(pieces) + 1) + [whole(cotangent.shape)],
            out_specs=(whole(cotangent.shape), *(anywhere,) * 4)
            + (whole((row_blocks, tok_rows, BLOCK)),),
            scratch_shapes=[
                pltpu.VMEM((row_blocks, tok_rows, BLOCK), BF16),
                pltpu.VMEM((row_blocks, BLOCK, tok_rows), BF16),
                pltpu.VMEM((row_blocks, tok_rows, BLOCK), F32),
                pltpu.VMEM((groups, used, part, BLOCK), BF16),
                pltpu.VMEM((2, 4, used, part, BLOCK), BF16),
                pltpu.VMEM((2 * panels, tok_rows, BLOCK), BF16),
                pltpu.SemaphoreType.DMA((sides, ring)),
                pltpu.SemaphoreType.DMA((2, panels)),
                pltpu.SemaphoreType.DMA((2, 2, panels)),
            ],
        ),
        compiler_params=alone,
        name="gated_pair",
    )(table, count, where, *pieces, held, cotangent)

    def around(value, s):
        pairs = [(y * 2 + c, (y + s) % 4 * 2 + c) for y in range(4) for c in range(2)]
        return lax.ppermute(value, "dp", pairs)

    piece = jax.ShapeDtypeStruct((used // 2, part, BLOCK), BF16)

    def reduced(mine, other):
        block = pl.BlockSpec((4, MOST, part, BLOCK), lambda i, w: (0, i, 0, 0))
        return pl.pallas_call(
            core_kernel,
            out_shape=(piece,) * 4,
            grid_spec=pltpu.PrefetchScalarGridSpec(
                num_scalar_prefetch=1,
                grid=(panels,),
                in_specs=[block] * 2,
                out_specs=(pl.BlockSpec((MOST, part, BLOCK), lambda i, w: (i, 0, 0)),) * 4,
            ),
            compiler_params=params,
            name="core_sum",
        )(where, mine, other)

    def swap(value):
        return lax.ppermute(value, "dp", [(d, d ^ 1) for d in range(groups)])

    mine = [mine_g, mine_u]
    other = [swap(other_g), swap(other_u)]
    sent = [reduced(mine[m], other[m]) for m in range(2)]
    middle = used // 4
    passed = [(around(sent[m][2][:middle], 1), around(sent[m][2][middle:], 3)) for m in range(2)]
    came = []
    for m in range(2):
        near, back = pl.pallas_call(
            relay_kernel,
            out_shape=(piece, piece),
            compiler_params=params,
            name="relay",
        )(sent[m][1], sent[m][3], *passed[m])
        came.append([sent[m][0], around(near, 1), around(back, 3)])
    columns = [[x * ring + z for x in range(sides)] for z in range(ring)]
    row_terms = lax.psum_scatter(
        terms, "mp", scatter_dimension=0, axis_index_groups=columns, tiled=True
    )
    returning = pl.pallas_call(
        unsort_kernel,
        out_shape=jax.ShapeDtypeStruct((slots, part, BLOCK), BF16),
        grid_spec=pltpu.PrefetchScalarGridSpec(
            num_scalar_prefetch=2,
            grid=(1,),
            in_specs=[whole(piece.shape)] * 6,
            out_specs=whole((slots, part, BLOCK)),
        ),
        compiler_params=less,
        name="unsort_slots",
    )(table, count, *came[0], *came[1])
    own = pl.pallas_call(
        lambda *refs: own_kernel(panels, *refs),
        out_shape=jax.ShapeDtypeStruct((2, owned, part, BLOCK), BF16),
        grid_spec=pltpu.PrefetchScalarGridSpec(
            num_scalar_prefetch=2,
            grid=(1,),
            in_specs=[whole((slots, part, BLOCK))],
            out_specs=whole((2, owned, part, BLOCK)),
        ),
        compiler_params=params,
        name="own_slots",
    )(where, tile_cols, exchange(returning))
    own = own.reshape(2 * owned, part, BLOCK)
    far, near, back = (around(own, s) for s in (2, 1, 3))
    full = [own, near, far, back]
    full = [v for t in full for v in (t, swap(t))]
    input_grad = lax.psum_scatter(
        row_terms, "mp", scatter_dimension=0, axis_index_groups=rows, tiled=True
    )
    tile_grads, input_grad = pl.pallas_call(
        widen_kernel,
        out_shape=(
            jax.ShapeDtypeStruct((2 * owned, BLOCK, BLOCK), F32),
            jax.ShapeDtypeStruct(tokens.shape, BF16),
        ),
        grid_spec=pltpu.PrefetchScalarGridSpec(
            num_scalar_prefetch=1,
            grid=(1,),
            in_specs=[whole((2 * owned, part, BLOCK))] * groups
            + [anywhere],
            out_specs=(anywhere, anywhere),
            scratch_shapes=[
                pltpu.VMEM((2 * owned, BLOCK, BLOCK), F32),
                pltpu.SemaphoreType.DMA((6,)),
                pltpu.SemaphoreType.DMA((my_blocks,)),
            ],
        ),
        compiler_params=less,
        name="widen",
    )(where, *full, input_grad)
    tile_grads = tile_grads.reshape(tiles.shape)
    return hidden, input_grad, tile_grads


def solution(mesh):
    in_specs = (P("dp", "mp"), P("dp", "mp"), P(None, "mp", None, None), P(), P())
    out_specs = (P("dp", "mp"), P("dp", "mp"), P(None, "mp", None, None))
    return jax.shard_map(
        per_device, mesh=mesh, in_specs=in_specs, out_specs=out_specs, check_vma=False
    )
```

```python
import jax
import jax.numpy as jnp
from jax import lax
from jax.experimental import pallas as pl
from jax.experimental.pallas import tpu as pltpu
from jax.sharding import PartitionSpec as P

BLOCK = 128
MOST = 12
PAIR = 3
GROUP = 4
F32 = jnp.float32
BF16 = jnp.bfloat16


def nt(a, b):
    return lax.dot_general(a, b, (((1,), (1,)), ((), ())), preferred_element_type=F32)


def nn(a, b):
    return lax.dot_general(a, b, (((1,), (0,)), ((), ())), preferred_element_type=F32)


def slot_table(tile_rows, tile_cols, me, members, panels):
    owned = tile_cols.shape[1] // members
    cols = tile_cols.reshape(2, members, owned)
    rows = tile_rows.reshape(2, members, owned)
    local = cols - me * panels
    holder = cols // panels
    pad = jnp.full((2, members, 2), -1, jnp.int32)

    def run(values):
        one = jnp.concatenate([pad[:, :, :1], values[:, :, :-1]], axis=2)
        two = jnp.concatenate([pad, values[:, :, :-2]], axis=2)
        return (values == one).astype(jnp.int32) + (values == two).astype(jnp.int32)

    rank = run(holder)
    within = run(cols)
    value = jnp.arange(members)[None, :, None] * 256 + rank * 64 + rows
    mine = local[None] == jnp.arange(panels)[:, None, None, None]
    count = jnp.sum(mine.astype(jnp.int32), axis=3)
    before = jnp.arange(members)[:, None] > jnp.arange(members)[None, :]
    earlier = jnp.sum(jnp.where(before, count[:, :, None, :], 0), axis=3)
    place_in_panel = jnp.where(mine, earlier[..., None] + within[None], -1)
    hit = place_in_panel[:, :, None] == jnp.arange(MOST)[:, None, None]
    table = jnp.sum(jnp.where(hit, value[None, :, None], 0), axis=(3, 4))
    return jnp.swapaxes(table, 0, 1).reshape(-1), jnp.sum(count, axis=2).T.reshape(-1)


def slot_of(cols_ref, me, owned, panels, m, visit):
    by = 65536 // panels + 1

    def step(k, carry):
        last, rank = carry
        holder = (cols_ref[m, me * owned + k] * by) >> 16
        rank = jnp.where(holder == last, rank + 1, 0)
        visit(k, holder, rank)
        return holder, rank

    lax.fori_loop(0, owned, step, (jnp.int32(-1), jnp.int32(0)), unroll=7)


def send_kernel(panels, cols_ref, tiles_ref, tokens_ref, out_ref, blocks_ref):
    for m in range(2):

        def visit(k, holder, rank):
            out_ref[holder * (2 * PAIR) + m * PAIR + rank] = tiles_ref[m, k]

        slot_of(cols_ref, lax.axis_index("mp"), tiles_ref.shape[1], panels, m, visit)
    for b in range(blocks_ref.shape[0]):
        blocks_ref[b] = tokens_ref[:, b * BLOCK : (b + 1) * BLOCK]


def own_kernel(panels, place_ref, cols_ref, back_ref, out_ref):
    for m in range(2):

        def visit(k, holder, rank):
            out_ref[m, k] = back_ref[holder * (2 * PAIR) + m * PAIR + rank]

        slot_of(cols_ref, place_ref[0], out_ref.shape[1], panels, m, visit)


def sort_kernel(table_ref, in_ref, out_ref):
    half = out_ref.shape[0] // 2
    for m in range(2):

        def step(s, carry):
            v = table_ref[m * half + s]
            out_ref[m * half + s] = in_ref[(v >> 8) * (2 * PAIR) + m * PAIR + ((v >> 6) & 3)]
            return carry

        lax.fori_loop(0, half, step, 0, unroll=6)


def unsort_kernel(table_ref, count_ref, *refs):
    out_ref = refs[-1]
    each = len(refs) // 2
    half = refs[0].shape[0]
    panels = half // MOST
    for m in range(2):
        in_refs = refs[m * each : (m + 1) * each]
        for q in range(panels):

            def step(g, carry):
                for i in range(GROUP):
                    s = q * MOST + g * GROUP + i
                    v = table_ref[m * half + s]
                    total = sum(r[s].astype(F32) for r in in_refs).astype(BF16)
                    out_ref[(v >> 8) * (2 * PAIR) + m * PAIR + ((v >> 6) & 3)] = total
                return carry

            lax.fori_loop(0, count_ref[m * panels + q] // GROUP, step, 0)


def core_kernel(where_ref, mine_ref, other_ref, *out_refs):
    for k, out_ref in enumerate(out_refs):
        y = lax.rem(where_ref[5] + k, 4)
        out_ref[...] = (mine_ref[y].astype(F32) + other_ref[y].astype(F32)).astype(BF16)


def relay_kernel(near_ref, back_ref, first_ref, last_ref, near_out, back_out):
    half = first_ref.shape[0]
    near_out[:half] = (near_ref[:half].astype(F32) + first_ref[...].astype(F32)).astype(BF16)
    near_out[half:] = near_ref[half:]
    back_out[:half] = back_ref[:half]
    back_out[half:] = (back_ref[half:].astype(F32) + last_ref[...].astype(F32)).astype(BF16)


def main_kernel(sides, ring, panels, table_ref, count_ref, where_ref, *refs):
    pieces, refs = refs[: ring + 1], refs[ring + 1 :]
    tile_hbm, cot_ref, hidden_ref, *refs = refs
    grads_hbm, refs = (refs[:2], refs[2:4]), refs[4:]
    terms_ref, tok_ref, tok_t, total, tile_ref, grad_ref, pair_ref, *refs = refs
    tok_sems, in_sems, out_sems = refs
    blocks = tok_ref.shape[0]
    each = blocks // sides
    turned = -(-blocks // panels)
    side = where_ref[2]

    core = where_ref[4]

    def loads(p):
        for m in range(2):
            at = pl.ds((m * panels + p) * MOST, MOST)
            yield pltpu.make_async_copy(tile_hbm.at[:, at], tile_ref.at[:, at], in_sems.at[m, p])

    def stores(p):
        for m in range(2):
            at, to = pl.ds((m * panels + p) * MOST, MOST), pl.ds(p * MOST, MOST)
            for k in range(2):
                yield pltpu.make_async_copy(
                    grad_ref.at[k, :, at], grads_hbm[k][m].at[:, to], out_sems.at[k, m, p]
                )

    steps = [j for j in range(ring) if j != ring // 2]
    held = [(j, s, piece.at[s]) for j, piece in zip(steps, pieces) for s in range(sides)]
    held += [
        (ring // 2, k * sides // 2 + s, piece.at[s])
        for k, piece in enumerate(pieces[-2:])
        for s in range(sides // 2)
    ]
    copies = [
        pltpu.make_async_copy(
            piece,
            tok_ref.at[
                pl.ds(
                    lax.rem(side + sides - s, sides) * each
                    + lax.rem(where_ref[3] + ring - j, ring) * (each // ring),
                    each // ring,
                )
            ],
            tok_sems.at[s, j],
        )
        for j, s, piece in held
    ]
    for copy in copies:
        copy.start()
    for p in range(panels):
        for copy in loads(p):
            copy.start()

    def clear(b, carry):
        total[b] = jnp.zeros_like(total[b])
        return carry

    lax.fori_loop(0, blocks, clear, 0)
    for copy in copies:
        copy.wait()

    def stacked(p, m, first):
        w = tile_ref[:, pl.ds((m * panels + p) * MOST + first, GROUP)]
        return jnp.concatenate([w[:, i].reshape(BLOCK, BLOCK) for i in range(GROUP)], axis=0)

    def by_counts(p, work):
        many = [count_ref[m * panels + p] > GROUP for m in range(2)]
        for most in range(4):
            picked = [bool(most & 1), bool(most & 2)]
            same = [many[m] if picked[m] else jnp.logical_not(many[m]) for m in range(2)]

            @pl.when(jnp.logical_and(same[0], same[1]))
            def _():
                counts = [MOST if picked[m] else GROUP for m in range(2)]
                at = [
                    [table_ref[(m * panels + p) * MOST + t] & 63 for t in range(counts[m])]
                    for m in range(2)
                ]
                work(p, counts, at)

    def forward(p, counts, at):
        for i in range(turned):
            b = jnp.minimum(p * turned + i, blocks - 1)
            tok_t[b] = tok_ref[b].T
        pre = []
        for m in range(2):
            acc = None
            for first in range(0, counts[m], GROUP):
                lhs = jnp.concatenate([tok_ref[at[m][first + i]] for i in range(GROUP)], axis=1)
                term = nn(lhs, stacked(p, m, first))
                acc = term if acc is None else acc + term
            pre.append(acc)
        gate, up = pre
        sig = 1.0 / (1.0 + jnp.exp(-gate))
        columns = pl.ds(pl.multiple_of(p * BLOCK, BLOCK), BLOCK)
        hidden_ref[:, columns] = (gate * sig * up).astype(BF16)
        cot = cot_ref[:, columns].astype(F32)
        pair_ref[p * 2] = (cot * up * sig * (1.0 + gate * (1.0 - sig))).astype(BF16)
        pair_ref[p * 2 + 1] = (cot * gate * sig).astype(BF16)

    def backward(p, counts, at):
        for m in range(2):
            grad = pair_ref[p * 2 + m]
            for first in range(0, counts[m], GROUP):
                lhs = jnp.concatenate([tok_t[at[m][first + i]] for i in range(GROUP)], axis=0)
                out = nn(lhs, grad).astype(BF16)
                back = nt(grad, stacked(p, m, first))
                for i in range(GROUP):
                    part = out[i * BLOCK : (i + 1) * BLOCK].reshape(4, 2, BLOCK // 8, BLOCK)
                    slot = (m * panels + p) * MOST + first + i
                    grad_ref[core, :, slot] = part[:, 0]
                    grad_ref[1 - core, :, slot] = part[:, 1]
                    total[at[m][first + i]] += back[:, i * BLOCK : (i + 1) * BLOCK]

    def first_pass(p, carry):
        for copy in loads(p):
            copy.wait()
        by_counts(p, forward)
        return carry

    def second_pass(p, carry):
        by_counts(p, backward)
        for copy in stores(p):
            copy.start()
        return carry

    lax.fori_loop(0, panels, first_pass, 0)
    lax.fori_loop(0, panels, second_pass, 0)

    def step(b, carry):
        terms_ref[b] = total[b].astype(BF16)
        return carry

    lax.fori_loop(0, blocks, step, 0, unroll=2)
    for p in range(panels):
        for copy in stores(p):
            copy.wait()


def widen_kernel(where_ref, *refs):
    pieces, (blocks_hbm, out_hbm, flat_hbm, out_ref, sems, flat_sems) = refs[:-6], refs[-6:]
    count, part, _ = pieces[0].shape
    stores = sems.shape[0]
    some = count // stores
    core, y = where_ref[4], where_ref[5]

    def store(i):
        at = pl.ds(i * some, some)
        return pltpu.make_async_copy(out_ref.at[at], out_hbm.at[at], sems.at[i])

    flat = [
        pltpu.make_async_copy(
            blocks_hbm.at[b], flat_hbm.at[:, pl.ds(b * BLOCK, BLOCK)], flat_sems.at[b]
        )
        for b in range(flat_sems.shape[0])
    ]
    for copy in flat:
        copy.start()
    for i in range(stores):
        for k, piece in enumerate(pieces):
            chunk = lax.rem(y + 4 - k // 2, 4) * 2 + (1 - core if k % 2 else core)
            rows = pl.ds(pl.multiple_of(chunk * part, part), part)
            out_ref[i * some : (i + 1) * some, rows, :] = piece[i * some : (i + 1) * some].astype(F32)
        store(i).start()
    for i in range(stores):
        store(i).wait()
    for copy in flat:
        copy.wait()


def whole(shape):
    return pl.BlockSpec(shape, lambda *_: (0,) * len(shape))


def per_device(tokens, cotangent, tiles, tile_rows, tile_cols):
    groups = lax.axis_size("dp")
    members = lax.axis_size("mp")
    me = lax.axis_index("mp")
    mygroup = lax.axis_index("dp")
    owned = tiles.shape[1]
    tok_rows, my_features = tokens.shape
    my_blocks = my_features // BLOCK
    row_blocks = my_blocks * members
    panels = cotangent.shape[1] // BLOCK
    part = BLOCK // groups
    slots = members * 2 * PAIR
    used = panels * 2 * MOST
    params = pltpu.CompilerParams(vmem_limit_bytes=48 * 1024 * 1024)
    less = pltpu.CompilerParams(vmem_limit_bytes=24 * 1024 * 1024)
    alone = pltpu.CompilerParams(vmem_limit_bytes=60 * 1024 * 1024)
    sides = 4
    ring = members // sides
    each = row_blocks // sides
    where = jnp.stack([me, mygroup, me // ring, me % ring, mygroup % 2, mygroup // 2]).astype(jnp.int32)

    outgoing, my_tok = pl.pallas_call(
        lambda *refs: send_kernel(panels, *refs),
        out_shape=(
            jax.ShapeDtypeStruct((slots, part, BLOCK), BF16),
            jax.ShapeDtypeStruct((my_blocks, tok_rows, BLOCK), BF16),
        ),
        grid_spec=pltpu.PrefetchScalarGridSpec(
            num_scalar_prefetch=1,
            grid=(1,),
            in_specs=[
                pl.BlockSpec((2, owned, part, BLOCK), lambda i, c: (0, 0, lax.axis_index("dp"), 0)),
                whole(tokens.shape),
            ],
            out_specs=(whole((slots, part, BLOCK)), whole((my_blocks, tok_rows, BLOCK))),
        ),
        compiler_params=alone,
        name="send_pack",
    )(tile_cols, tiles, tokens)

    def exchange(values):
        shape = (members, -1) + values.shape[1:]
        return lax.all_to_all(values.reshape(shape), "mp", 0, 0).reshape(values.shape)

    rows = [[x * ring + z for z in range(ring)] for x in range(sides)]

    def turn(value, s):
        pairs = [
            (x * ring + z, (x + s) % sides * ring + z) for x in range(sides) for z in range(ring)
        ]
        return lax.ppermute(value, "mp", pairs)

    def along(value, s):
        pairs = [
            (x * ring + z, x * ring + (z + s) % ring) for x in range(sides) for z in range(ring)
        ]
        return lax.ppermute(value, "mp", pairs)

    line_tok = jnp.stack([my_tok] + [turn(my_tok, s) for s in range(1, sides)])
    table, count = slot_table(tile_rows, tile_cols, me, members, panels)
    incoming, line_tok = lax.optimization_barrier((exchange(outgoing), line_tok))
    ordered = pl.pallas_call(
        sort_kernel,
        out_shape=jax.ShapeDtypeStruct((used, part, BLOCK), BF16),
        grid_spec=pltpu.PrefetchScalarGridSpec(
            num_scalar_prefetch=1,
            grid=(1,),
            in_specs=[whole((slots, part, BLOCK))],
            out_specs=whole((used, part, BLOCK)),
        ),
        compiler_params=params,
        name="sort_slots",
    )(table, incoming)
    held = lax.all_gather(ordered, "dp")
    ups, downs = [line_tok], [line_tok]
    for _ in range(ring // 2 - 1):
        ups.append(along(ups[-1], 1))
        downs.append(along(downs[-1], -1))
    far = [along(ups[-1][: sides // 2], 1), along(downs[-1][sides // 2 :], -1)]
    pieces = ups + downs[:0:-1] + far

    anywhere = pl.BlockSpec(memory_space=pl.ANY)
    split = jax.ShapeDtypeStruct((4, used // 2, part, BLOCK), BF16)
    hidden, mine_g, mine_u, other_g, other_u, terms = pl.pallas_call(
        lambda *refs: main_kernel(sides, ring, panels, *refs),
        out_shape=(
            jax.ShapeDtypeStruct(cotangent.shape, BF16),
            *(split,) * 4,
        )
        + (jax.ShapeDtypeStruct((row_blocks, tok_rows, BLOCK), BF16),),
        grid_spec=pltpu.PrefetchScalarGridSpec(
            num_scalar_prefetch=3,
            grid=(1,),
            in_specs=[anywhere] * (len(pieces) + 1) + [whole(cotangent.shape)],
            out_specs=(whole(cotangent.shape), *(anywhere,) * 4)
            + (whole((row_blocks, tok_rows, BLOCK)),),
            scratch_shapes=[
                pltpu.VMEM((row_blocks, tok_rows, BLOCK), BF16),
                pltpu.VMEM((row_blocks, BLOCK, tok_rows), BF16),
                pltpu.VMEM((row_blocks, tok_rows, BLOCK), F32),
                pltpu.VMEM((groups, used, part, BLOCK), BF16),
                pltpu.VMEM((2, 4, used, part, BLOCK), BF16),
                pltpu.VMEM((2 * panels, tok_rows, BLOCK), BF16),
                pltpu.SemaphoreType.DMA((sides, ring)),
                pltpu.SemaphoreType.DMA((2, panels)),
                pltpu.SemaphoreType.DMA((2, 2, panels)),
            ],
        ),
        compiler_params=alone,
        name="gated_pair",
    )(table, count, where, *pieces, held, cotangent)

    def around(value, s):
        pairs = [(y * 2 + c, (y + s) % 4 * 2 + c) for y in range(4) for c in range(2)]
        return lax.ppermute(value, "dp", pairs)

    piece = jax.ShapeDtypeStruct((used // 2, part, BLOCK), BF16)

    def reduced(mine, other):
        block = pl.BlockSpec((4, MOST, part, BLOCK), lambda i, w: (0, i, 0, 0))
        return pl.pallas_call(
            core_kernel,
            out_shape=(piece,) * 4,
            grid_spec=pltpu.PrefetchScalarGridSpec(
                num_scalar_prefetch=1,
                grid=(panels,),
                in_specs=[block] * 2,
                out_specs=(pl.BlockSpec((MOST, part, BLOCK), lambda i, w: (i, 0, 0)),) * 4,
            ),
            compiler_params=params,
            name="core_sum",
        )(where, mine, other)

    def swap(value):
        return lax.ppermute(value, "dp", [(d, d ^ 1) for d in range(groups)])

    mine = [mine_g, mine_u]
    other = [swap(other_g), swap(other_u)]
    sent = [reduced(mine[m], other[m]) for m in range(2)]
    middle = used // 4
    passed = [(around(sent[m][2][:middle], 1), around(sent[m][2][middle:], 3)) for m in range(2)]
    came = []
    for m in range(2):
        near, back = pl.pallas_call(
            relay_kernel,
            out_shape=(piece, piece),
            compiler_params=params,
            name="relay",
        )(sent[m][1], sent[m][3], *passed[m])
        came.append([sent[m][0], around(near, 1), around(back, 3)])
    columns = [[x * ring + z for x in range(sides)] for z in range(ring)]
    row_terms = lax.psum_scatter(
        terms, "mp", scatter_dimension=0, axis_index_groups=columns, tiled=True
    )
    returning = pl.pallas_call(
        unsort_kernel,
        out_shape=jax.ShapeDtypeStruct((slots, part, BLOCK), BF16),
        grid_spec=pltpu.PrefetchScalarGridSpec(
            num_scalar_prefetch=2,
            grid=(1,),
            in_specs=[whole(piece.shape)] * 6,
            out_specs=whole((slots, part, BLOCK)),
        ),
        compiler_params=less,
        name="unsort_slots",
    )(table, count, *came[0], *came[1])
    own = pl.pallas_call(
        lambda *refs: own_kernel(panels, *refs),
        out_shape=jax.ShapeDtypeStruct((2, owned, part, BLOCK), BF16),
        grid_spec=pltpu.PrefetchScalarGridSpec(
            num_scalar_prefetch=2,
            grid=(1,),
            in_specs=[whole((slots, part, BLOCK))],
            out_specs=whole((2, owned, part, BLOCK)),
        ),
        compiler_params=params,
        name="own_slots",
    )(where, tile_cols, exchange(returning))
    own = own.reshape(2 * owned, part, BLOCK)
    near, back = around(own, 1), around(own, 3)
    far = jnp.concatenate([around(near[:owned], 1), around(back[owned:], 3)], axis=0)
    full = [own, near, far, back]
    full = [v for t in full for v in (t, swap(t))]
    input_grad = lax.psum_scatter(
        row_terms, "mp", scatter_dimension=0, axis_index_groups=rows, tiled=True
    )
    tile_grads, input_grad = pl.pallas_call(
        widen_kernel,
        out_shape=(
            jax.ShapeDtypeStruct((2 * owned, BLOCK, BLOCK), F32),
            jax.ShapeDtypeStruct(tokens.shape, BF16),
        ),
        grid_spec=pltpu.PrefetchScalarGridSpec(
            num_scalar_prefetch=1,
            grid=(1,),
            in_specs=[whole((2 * owned, part, BLOCK))] * groups
            + [anywhere],
            out_specs=(anywhere, anywhere),
            scratch_shapes=[
                pltpu.VMEM((2 * owned, BLOCK, BLOCK), F32),
                pltpu.SemaphoreType.DMA((6,)),
                pltpu.SemaphoreType.DMA((my_blocks,)),
            ],
        ),
        compiler_params=less,
        name="widen",
    )(where, *full, input_grad)
    tile_grads = tile_grads.reshape(tiles.shape)
    return hidden, input_grad, tile_grads


def solution(mesh):
    in_specs = (P("dp", "mp"), P("dp", "mp"), P(None, "mp", None, None), P(), P())
    out_specs = (P("dp", "mp"), P("dp", "mp"), P(None, "mp", None, None))
    return jax.shard_map(
        per_device, mesh=mesh, in_specs=in_specs, out_specs=out_specs, check_vma=False
    )
```
